256 devices in a mesh: sec: 2 (over core), row: 16 (over x, y), col: 8 (over z).
Axes of the slice: x: 4, y: 4, z: 8, core: 2. Of those that a mesh axis runs over, the one named last changes fastest.
Arguments:
- images: bfloat16 [2, 256, 256, 384], P('sec', 'row', 'col'), may hold values from -6 to 6
- kernel_one: float32 [49, 384], replicated, may hold values from -0.875 to 0.875
- gain_one: float32 [384], replicated, may hold values from 0.5 to 1.5
- shift_one: float32 [384], replicated, may hold values from -3 to 3
- up_one: bfloat16 [384, 1536], P(None, ('sec', 'row', 'col')), may hold values from -0.3125 to 0.3125
- up_bias_one: float32 [1536], replicated, may hold values from -3 to 3
- down_one: bfloat16 [384, 1536], P(None, ('sec', 'row', 'col')), may hold values from -0.15625 to 0.15625
- down_bias_one: float32 [384], replicated, may hold values from -3 to 3
- scale_one: float32 [384], replicated, may hold values from 0.3 to 1.5
- gain_mid: float32 [384], replicated, may hold values from 0.5 to 1.5
- shift_mid: float32 [384], replicated, may hold values from -3 to 3
- merge_weight: bfloat16 [1536, 768], replicated, may hold values from -0.15625 to 0.15625
- merge_bias: float32 [768], replicated, may hold values from -3 to 3
- kernel_two: float32 [49, 768], replicated, may hold values from -0.875 to 0.875
- gain_two: float32 [768], replicated, may hold values from 0.5 to 1.5
- shift_two: float32 [768], replicated, may hold values from -3 to 3
- up_two: bfloat16 [768, 3072], P(None, ('sec', 'row', 'col')), may hold values from -0.21875 to 0.21875
- up_bias_two: float32 [3072], replicated, may hold values from -3 to 3
- down_two: bfloat16 [768, 3072], P(None, ('sec', 'row', 'col')), may hold values from -0.109375 to 0.109375
- down_bias_two: float32 [768], replicated, may hold values from -3 to 3
- scale_two: float32 [768], replicated, may hold values from 0.3 to 1.5
- grad_out: bfloat16 [2, 128, 128, 768], P('sec', 'row', 'col'), may hold values from -6 to 6
Outputs:
- features: bfloat16 [2, 128, 128, 768], P('sec', 'row', 'col')
- input_grad: bfloat16 [2, 256, 256, 384], P('sec', 'row', 'col')
The draws below stay inside these ranges and needn't reach their ends.
All inputs are finite; a program needn't handle non-finite values.
Results may differ from the reference program's by a relative error of at most 0.02.
Values may be sent and summed in bfloat16 or wider, within the bound.
No kernel may reach another device: no remote copies, remote signals or barrier semaphores. Data moves between devices by JAX's collectives and lax.ppermute only.
A program may use at most 128 MiB of HBM per device.

```python
import math
import jax
import jax.numpy as jnp
from jax import lax

C1 = 384
C2 = 768
FF1 = 1536
FF2 = 3072
MB = 2
H = 256
W = 256
H2 = 128
W2 = 128


def steps_of(own_key, extent, pieces, low, top_value):
    factor_of, own = 1.0, jax.random.fold_in(own_key, 6)
    for position, shards_of in pieces:
        heights = jnp.exp(jax.random.uniform(jax.random.fold_in(own, position), (shards_of,), jnp.float32, low / len(pieces), top_value / len(pieces)))
        factor_of = factor_of * jnp.repeat(heights, extent[position] // shards_of).reshape([-1 if axis == position else 1 for axis in range(len(extent))])
    return factor_of


def normal_values(key, dims, spread, reach, shards=(), dtype=jnp.bfloat16):
    gain = steps_of(key, dims, shards, -0.22, 0.18) if shards else 1.0
    array = jax.random.normal(key, dims, jnp.float32) * spread * gain
    return jnp.minimum(jnp.maximum(array, -reach), reach).astype(dtype)


def setup_inputs(seed: int = 0) -> dict:
    arg_keys = jax.random.split(jax.random.key(seed), 23)
    return {
        "images": normal_values(arg_keys[0], (MB, H, W, C1), 1.0, 6.0, ((0, 2), (1, 16), (2, 8))),
        "kernel_one": normal_values(arg_keys[1], (49, C1), 49 ** -0.5, 0.875, (), jnp.float32),
        "gain_one": jnp.clip(1.0 + 0.1 * jax.random.normal(arg_keys[2], (C1,), jnp.float32), 0.5, 1.5),
        "shift_one": normal_values(arg_keys[3], (C1,), 0.5, 3.0, (), jnp.float32),
        "up_one": normal_values(arg_keys[4], (C1, FF1), C1 ** -0.5, 0.3125, ((1, 256),)),
        "up_bias_one": normal_values(arg_keys[5], (FF1,), 0.5, 3.0, (), jnp.float32),
        "down_one": normal_values(arg_keys[6], (C1, FF1), FF1 ** -0.5, 0.15625, ((1, 256),)),
        "down_bias_one": normal_values(arg_keys[7], (C1,), 0.5, 3.0, (), jnp.float32),
        "scale_one": jnp.clip(jnp.exp(jax.random.uniform(arg_keys[8], (C1,), jnp.float32, math.log(0.3), math.log(1.5))), 0.3, 1.5),
        "gain_mid": jnp.clip(1.0 + 0.1 * jax.random.normal(arg_keys[9], (C1,), jnp.float32), 0.5, 1.5),
        "shift_mid": normal_values(arg_keys[10], (C1,), 0.5, 3.0, (), jnp.float32),
        "merge_weight": normal_values(arg_keys[11], (4 * C1, C2), (4 * C1) ** -0.5, 0.15625),
        "merge_bias": normal_values(arg_keys[12], (C2,), 0.5, 3.0, (), jnp.float32),
        "kernel_two": normal_values(arg_keys[13], (49, C2), 49 ** -0.5, 0.875, (), jnp.float32),
        "gain_two": jnp.clip(1.0 + 0.1 * jax.random.normal(arg_keys[14], (C2,), jnp.float32), 0.5, 1.5),
        "shift_two": normal_values(arg_keys[15], (C2,), 0.5, 3.0, (), jnp.float32),
        "up_two": normal_values(arg_keys[16], (C2, FF2), C2 ** -0.5, 0.21875, ((1, 256),)),
        "up_bias_two": normal_values(arg_keys[17], (FF2,), 0.5, 3.0, (), jnp.float32),
        "down_two": normal_values(arg_keys[18], (C2, FF2), FF2 ** -0.5, 0.109375, ((1, 256),)),
        "down_bias_two": normal_values(arg_keys[19], (C2,), 0.5, 3.0, (), jnp.float32),
        "scale_two": jnp.clip(jnp.exp(jax.random.uniform(arg_keys[20], (C2,), jnp.float32, math.log(0.3), math.log(1.5))), 0.3, 1.5),
        "grad_out": normal_values(arg_keys[21], (MB, H2, W2, C2), 1.0, 6.0, ((0, 2), (1, 16), (2, 8))),
    }


norm_eps = 1e-06

def gelu_exact(values):
    return 0.5 * values * (1.0 + lax.erf(values * 0.7071067811865476))

def gelu_slope(values):
    return 0.5 * (1.0 + lax.erf(values * 0.7071067811865476)) + values * jnp.exp(-0.5 * values * values) * 0.3989422804014327

def norm_forward(values, norm_gain, norm_shift):
    center = values - lax.optimization_barrier(jnp.mean(values, axis=-1, keepdims=True))
    inv_std = lax.rsqrt(lax.optimization_barrier(jnp.mean(center * center, axis=-1, keepdims=True)) + norm_eps)
    scaled = center * inv_std
    return (scaled, inv_std, scaled * norm_gain + norm_shift)

def norm_backward(upstream, scaled, inv_std, norm_gain):
    weighted = upstream * norm_gain
    mean_one = lax.optimization_barrier(jnp.mean(weighted, axis=-1, keepdims=True))
    mean_two = lax.optimization_barrier(jnp.mean(weighted * scaled, axis=-1, keepdims=True))
    return inv_std * (weighted - mean_one - scaled * mean_two)

def taps_last(padded, kernel, row_count, col_count, flipped):
    summed = jnp.zeros(padded.shape[:-3] + (row_count, col_count, padded.shape[-1]), jnp.float32)
    for tap_index in range(49):
        row_off = tap_index // 7
        col_off = tap_index % 7
        if flipped:
            row_off = 6 - row_off
            col_off = 6 - col_off
        summed = summed + padded[..., row_off:row_off + row_count, col_off:col_off + col_count, :] * kernel[tap_index]
    return summed

def pad_grid(values):
    return jnp.pad(values, ((3, 3), (3, 3), (0, 0)))

def mlp_forward(normed, up_full, down_full, up_bias, down_bias):
    pre_act = jnp.dot(normed, up_full, preferred_element_type=jnp.float32) + up_bias
    hidden = gelu_exact(pre_act).astype(jnp.bfloat16)
    branch = jnp.dot(hidden, down_full.T, preferred_element_type=jnp.float32) + down_bias
    return (branch, pre_act)

def mlp_backward(d_branch, pre_act, up_full, down_full):
    d_hidden = jnp.dot(d_branch, down_full, preferred_element_type=jnp.float32)
    d_pre = (d_hidden * gelu_slope(pre_act)).astype(jnp.bfloat16)
    return jnp.dot(d_pre, up_full.T, preferred_element_type=jnp.float32)

def reference(images, kernel_one, gain_one, shift_one, up_one, up_bias_one, down_one, down_bias_one, scale_one, gain_mid, shift_mid, merge_weight, merge_bias, kernel_two, gain_two, shift_two, up_two, up_bias_two, down_two, down_bias_two, scale_two, grad_out):
    width_one = images.shape[-1]
    width_two = merge_weight.shape[1]

    def single(inputs_pair):
        sample, cotangent = inputs_pair
        grid_rows = sample.shape[0]
        grid_cols = sample.shape[1]
        half_rows = grid_rows // 2
        half_cols = grid_cols // 2
        conv_one = taps_last(pad_grid(sample.astype(jnp.float32)), kernel_one, grid_rows, grid_cols, False).reshape(-1, width_one)
        scaled_one, inv_one, normed_one = norm_forward(conv_one, gain_one, shift_one)
        normed_one = normed_one.astype(jnp.bfloat16)
        branch_one, pre_one = mlp_forward(normed_one, up_one, down_one, up_bias_one, down_bias_one)
        section_out = (sample.reshape(-1, width_one).astype(jnp.float32) + scale_one * branch_one).astype(jnp.bfloat16)
        scaled_mid, inv_mid, normed_mid = norm_forward(section_out.astype(jnp.float32), gain_mid, shift_mid)
        patches = normed_mid.astype(jnp.bfloat16).reshape(half_rows, 2, half_cols, 2, width_one).transpose(0, 2, 1, 3, 4).reshape(-1, 4 * width_one)
        merged = (jnp.dot(patches, merge_weight, preferred_element_type=jnp.float32) + merge_bias).astype(jnp.bfloat16)
        conv_two = taps_last(pad_grid(merged.reshape(half_rows, half_cols, width_two).astype(jnp.float32)), kernel_two, half_rows, half_cols, False).reshape(-1, width_two)
        conv_two = lax.optimization_barrier(conv_two.astype(jnp.bfloat16)).astype(jnp.float32)
        scaled_two, inv_two, normed_two = norm_forward(conv_two, gain_two, shift_two)
        normed_two = normed_two.astype(jnp.bfloat16)
        branch_two, pre_two = mlp_forward(normed_two, up_two, down_two, up_bias_two, down_bias_two)
        features = (merged.astype(jnp.float32) + scale_two * branch_two).astype(jnp.bfloat16)
        upstream_two = cotangent.reshape(-1, width_two).astype(jnp.float32)
        d_branch_two = (upstream_two * scale_two).astype(jnp.bfloat16)
        d_normed_two = mlp_backward(d_branch_two, pre_two, up_two, down_two)
        d_conv_two = norm_backward(d_normed_two, scaled_two, inv_two, gain_two).astype(jnp.bfloat16)
        back_two = taps_last(pad_grid(d_conv_two.reshape(half_rows, half_cols, width_two).astype(jnp.float32)), kernel_two, half_rows, half_cols, True).reshape(-1, width_two)
        back_two = lax.optimization_barrier(back_two.astype(jnp.bfloat16)).astype(jnp.float32)
        d_merged = (back_two + upstream_two).astype(jnp.bfloat16)
        d_patches = jnp.dot(d_merged, merge_weight.T, preferred_element_type=jnp.float32)
        d_normed_mid = d_patches.reshape(half_rows, half_cols, 2, 2, width_one).transpose(0, 2, 1, 3, 4).reshape(-1, width_one)
        upstream_one = norm_backward(d_normed_mid, scaled_mid, inv_mid, gain_mid)
        d_branch_one = (upstream_one * scale_one).astype(jnp.bfloat16)
        d_normed_one = mlp_backward(d_branch_one, pre_one, up_one, down_one)
        d_conv_one = norm_backward(d_normed_one, scaled_one, inv_one, gain_one).astype(jnp.bfloat16)
        back_one = taps_last(pad_grid(d_conv_one.reshape(grid_rows, grid_cols, width_one).astype(jnp.float32)), kernel_one, grid_rows, grid_cols, True).reshape(-1, width_one)
        input_grad = (back_one + upstream_one).astype(jnp.bfloat16).reshape(grid_rows, grid_cols, width_one)
        return (features.reshape(half_rows, half_cols, width_two), input_grad)
    features, input_grad = lax.map(single, (images, grad_out))
    return (features, input_grad)
```

```python
import jax
import jax.numpy as jnp
from jax import lax
from jax.sharding import PartitionSpec as P

norm_eps = 1e-06


def with_halo(block, sides, width):
    for axis, dim in sides:
        count = lax.axis_size(axis)
        forward = [(i, i + 1) for i in range(count - 1)]
        backward = [(target, source) for source, target in forward]
        low = lax.ppermute(
            lax.slice_in_dim(block, block.shape[dim] - width, None, axis=dim), axis, forward
        )
        high = lax.ppermute(lax.slice_in_dim(block, 0, width, axis=dim), axis, backward)
        block = jnp.concatenate([low, block, high], axis=dim)
    return block


def gelu_exact(values):
    return 0.5 * values * (1.0 + lax.erf(values * 0.7071067811865476))


def gelu_slope(values):
    return (
        0.5 * (1.0 + lax.erf(values * 0.7071067811865476))
        + values * jnp.exp(-0.5 * values * values) * 0.3989422804014327
    )


def norm_forward(values, norm_gain, norm_shift):
    center = values - jnp.mean(values, axis=-1, keepdims=True)
    inv_std = lax.rsqrt(jnp.mean(center * center, axis=-1, keepdims=True) + norm_eps)
    scaled = center * inv_std
    return (scaled, inv_std, scaled * norm_gain + norm_shift)


def norm_backward(upstream, scaled, inv_std, norm_gain):
    weighted = upstream * norm_gain
    mean_one = jnp.mean(weighted, axis=-1, keepdims=True)
    mean_two = jnp.mean(weighted * scaled, axis=-1, keepdims=True)
    return inv_std * (weighted - mean_one - scaled * mean_two)


def taps_last(padded, kernel, row_count, col_count, flipped):
    summed = jnp.zeros(padded.shape[:-3] + (row_count, col_count, padded.shape[-1]), jnp.float32)
    for tap_index in range(49):
        row_off = tap_index // 7
        col_off = tap_index % 7
        if flipped:
            row_off = 6 - row_off
            col_off = 6 - col_off
        summed = (
            summed
            + padded[..., row_off : row_off + row_count, col_off : col_off + col_count, :]
            * kernel[tap_index]
        )
    return summed


def contract_last(left_side, right_side):
    return lax.dot_general(
        left_side, right_side, (((1,), (1,)), ((), ())), preferred_element_type=jnp.float32
    )


def dense_forward(normed, weights, up_bias, down_bias):
    width = normed.shape[1]
    pre_acts = []
    branch = down_bias
    for part, part_bias in zip(weights, up_bias):
        pre_act = contract_last(normed, part[:, :width]) + part_bias
        hidden = gelu_exact(pre_act).astype(jnp.bfloat16)
        branch = branch + jnp.dot(hidden, part[:, width:], preferred_element_type=jnp.float32)
        pre_acts.append(pre_act)
    return (branch, pre_acts)


def dense_backward(d_branch, pre_acts, weights):
    width = d_branch.shape[1]
    total = 0.0
    for part, pre_act in zip(weights, pre_acts):
        d_hidden = contract_last(d_branch, part[:, width:])
        d_pre = (d_hidden * gelu_slope(pre_act)).astype(jnp.bfloat16)
        total = total + jnp.dot(d_pre, part[:, :width], preferred_element_type=jnp.float32)
    return total


def with_rims(tile_values):
    return with_halo(tile_values, (("row", 1), ("col", 2)), 3)


def on_device(
    images,
    kernel_one,
    gain_one,
    shift_one,
    up_one,
    up_bias_one,
    down_one,
    down_bias_one,
    scale_one,
    gain_mid,
    shift_mid,
    merge_weight,
    merge_bias,
    kernel_two,
    gain_two,
    shift_two,
    up_two,
    up_bias_two,
    down_two,
    down_bias_two,
    scale_two,
    grad_out,
):
    micro_count, tile_rows, tile_cols, width_one = images.shape
    width_two = merge_weight.shape[1]
    half_rows = tile_rows // 2
    half_cols = tile_cols // 2
    rows_one = micro_count * tile_rows * tile_cols
    rows_two = micro_count * half_rows * half_cols

    swap = [(0, 1), (1, 0)]
    side = lax.axis_index("sec")

    def both_halves(own):
        return (own, lax.ppermute(own, "sec", swap))

    def bias_halves(bias):
        halves = bias.reshape(2, -1)
        return (
            lax.dynamic_index_in_dim(halves, side, 0, keepdims=False),
            lax.dynamic_index_in_dim(halves, 1 - side, 0, keepdims=False),
        )

    share_one = up_one.shape[1]
    share_two = up_two.shape[1]
    packed = jnp.concatenate(
        [up_two.T, down_two.T, jnp.concatenate([up_one.T, down_one.T], axis=1)], axis=0
    )
    column = lax.all_gather(packed, "col", axis=0, tiled=False)
    part_one = column[:, 2 * share_two :].reshape(-1, 2 * width_one)
    part_two = jnp.concatenate(
        [
            column[:, :share_two].reshape(-1, width_two),
            column[:, share_two : 2 * share_two].reshape(-1, width_two),
        ],
        axis=1,
    )
    own_one = lax.all_gather(part_one, "row", axis=0, tiled=True)
    own_two = lax.all_gather(part_two, "row", axis=0, tiled=True)
    pair_one = both_halves(own_one)
    pair_two = both_halves(own_two)
    bias_one = bias_halves(up_bias_one)
    bias_two = bias_halves(up_bias_two)

    padded_one = with_rims(images).astype(jnp.float32)
    conv_one = taps_last(padded_one, kernel_one, tile_rows, tile_cols, False).reshape(
        rows_one, width_one
    )
    scaled_one, inv_one, normed_one = norm_forward(conv_one, gain_one, shift_one)
    normed_one = normed_one.astype(jnp.bfloat16)
    branch_one, pre_one = dense_forward(normed_one, pair_one, bias_one, down_bias_one)
    section_out = (
        images.reshape(rows_one, width_one).astype(jnp.float32) + scale_one * branch_one
    ).astype(jnp.bfloat16)
    scaled_mid, inv_mid, normed_mid = norm_forward(
        section_out.astype(jnp.float32), gain_mid, shift_mid
    )
    patches = normed_mid.astype(jnp.bfloat16).reshape(
        micro_count, half_rows, 2, half_cols, 2, width_one
    )
    patches = patches.transpose(0, 1, 3, 2, 4, 5).reshape(rows_two, 4 * width_one)
    merged = (
        jnp.dot(patches, merge_weight, preferred_element_type=jnp.float32) + merge_bias
    ).astype(jnp.bfloat16)
    merged_tile = merged.reshape(micro_count, half_rows, half_cols, width_two)
    padded_two = with_rims(merged_tile).astype(jnp.float32)
    conv_two = (
        taps_last(padded_two, kernel_two, half_rows, half_cols, False)
        .reshape(rows_two, width_two)
        .astype(jnp.bfloat16)
    )
    scaled_two, inv_two, normed_two = norm_forward(
        conv_two.astype(jnp.float32), gain_two, shift_two
    )
    normed_two = normed_two.astype(jnp.bfloat16)
    branch_two, pre_two = dense_forward(normed_two, pair_two, bias_two, down_bias_two)
    features = (merged.astype(jnp.float32) + scale_two * branch_two).astype(jnp.bfloat16)
    grad_rows = grad_out.reshape(rows_two, width_two)
    d_branch_two = (grad_rows.astype(jnp.float32) * scale_two).astype(jnp.bfloat16)
    d_normed_two = dense_backward(d_branch_two, pre_two, pair_two)
    d_conv_two = norm_backward(d_normed_two, scaled_two, inv_two, gain_two).astype(jnp.bfloat16)
    back_tile = d_conv_two.reshape(micro_count, half_rows, half_cols, width_two)
    padded_back = with_rims(back_tile).astype(jnp.float32)
    d_taps = (
        taps_last(padded_back, kernel_two, half_rows, half_cols, True)
        .reshape(rows_two, width_two)
        .astype(jnp.bfloat16)
    )
    d_taps = lax.optimization_barrier(d_taps).astype(jnp.float32)
    d_merged = (d_taps + grad_rows.astype(jnp.float32)).astype(jnp.bfloat16)
    d_patches = contract_last(d_merged, merge_weight)
    d_normed_mid = d_patches.reshape(micro_count, half_rows, half_cols, 2, 2, width_one)
    d_normed_mid = d_normed_mid.transpose(0, 1, 3, 2, 4, 5).reshape(rows_one, width_one)
    upstream_one = norm_backward(d_normed_mid, scaled_mid, inv_mid, gain_mid)
    d_branch_one = (upstream_one * scale_one).astype(jnp.bfloat16)
    d_normed_one = dense_backward(d_branch_one, pre_one, pair_one)
    d_conv_one = norm_backward(d_normed_one, scaled_one, inv_one, gain_one).astype(jnp.bfloat16)
    d_conv_one = d_conv_one.reshape(micro_count, tile_rows, tile_cols, width_one)
    padded_grad = with_rims(d_conv_one).astype(jnp.float32)
    back_one = taps_last(padded_grad, kernel_one, tile_rows, tile_cols, True).reshape(
        rows_one, width_one
    )
    input_grad = (back_one + upstream_one).astype(jnp.bfloat16).reshape(images.shape)
    return (features.reshape(micro_count, half_rows, half_cols, width_two), input_grad)


def solution(mesh):
    in_specs = (
        P("sec", "row", "col", None),
        P(),
        P(),
        P(),
        P(None, ("sec", "row", "col")),
        P(),
        P(None, ("sec", "row", "col")),
        P(),
        P(),
        P(),
        P(),
        P(),
        P(),
        P(),
        P(),
        P(),
        P(None, ("sec", "row", "col")),
        P(),
        P(None, ("sec", "row", "col")),
        P(),
        P(),
        P("sec", "row", "col", None),
    )
    out_specs = (P("sec", "row", "col", None), P("sec", "row", "col", None))
    return jax.shard_map(
        on_device, mesh=mesh, in_specs=in_specs, out_specs=out_specs, check_vma=False
    )
```

```python
import jax
import jax.numpy as jnp
from jax import lax
from jax.sharding import PartitionSpec as P

norm_eps = 1e-06


def with_halo(block, sides):
    for axis, dim, width in sides:
        count = lax.axis_size(axis)
        forward = [(i, i + 1) for i in range(count - 1)]
        backward = [(target, source) for source, target in forward]
        low = lax.ppermute(
            lax.slice_in_dim(block, block.shape[dim] - width, None, axis=dim), axis, forward
        )
        high = lax.ppermute(lax.slice_in_dim(block, 0, width, axis=dim), axis, backward)
        block = jnp.concatenate([low, block, high], axis=dim)
    return block


def ring_collect(piece, axis, inner, stride):
    count = lax.axis_size(axis)
    found = [piece]
    for shift in range(1, inner):
        pairs = []
        for target in range(count):
            place = (target // stride) % inner
            source = target + ((place + shift) % inner - place) * stride
            pairs.append((source, target))
        found.append(lax.ppermute(piece, axis, pairs))
    return jnp.concatenate(found, axis=0)


def gelu_exact(values):
    return 0.5 * values * (1.0 + lax.erf(values * 0.7071067811865476))


def gelu_slope(values):
    return (
        0.5 * (1.0 + lax.erf(values * 0.7071067811865476))
        + values * jnp.exp(-0.5 * values * values) * 0.3989422804014327
    )


def norm_forward(values, norm_gain, norm_shift):
    center = values - jnp.mean(values, axis=-1, keepdims=True)
    inv_std = lax.rsqrt(jnp.mean(center * center, axis=-1, keepdims=True) + norm_eps)
    scaled = center * inv_std
    return (scaled, inv_std, scaled * norm_gain + norm_shift)


def norm_backward(upstream, scaled, inv_std, norm_gain):
    weighted = upstream * norm_gain
    mean_one = jnp.mean(weighted, axis=-1, keepdims=True)
    mean_two = jnp.mean(weighted * scaled, axis=-1, keepdims=True)
    return inv_std * (weighted - mean_one - scaled * mean_two)


def taps_last(padded, kernel, row_count, col_count, flipped):
    summed = jnp.zeros(padded.shape[:-3] + (row_count, col_count, padded.shape[-1]), jnp.float32)
    for tap_index in range(49):
        row_off = tap_index // 7
        col_off = tap_index % 7
        if flipped:
            row_off = 6 - row_off
            col_off = 6 - col_off
        summed = (
            summed
            + padded[..., row_off : row_off + row_count, col_off : col_off + col_count, :]
            * kernel[tap_index]
        )
    return summed


def contract_last(left_side, right_side):
    return lax.dot_general(
        left_side, right_side, (((1,), (1,)), ((), ())), preferred_element_type=jnp.float32
    )


def dense_forward(normed, weights, up_bias, down_bias):
    width = normed.shape[1]
    pre_acts = []
    branch = down_bias
    for part, part_bias in zip(weights, up_bias):
        pre_act = contract_last(normed, part[:, :width]) + part_bias
        hidden = gelu_exact(pre_act).astype(jnp.bfloat16)
        branch = branch + jnp.dot(hidden, part[:, width:], preferred_element_type=jnp.float32)
        pre_acts.append(pre_act)
    return (branch, pre_acts)


def dense_backward(d_branch, pre_acts, weights):
    width = d_branch.shape[1]
    total = 0.0
    for part, pre_act in zip(weights, pre_acts):
        d_hidden = contract_last(d_branch, part[:, width:])
        d_pre = (d_hidden * gelu_slope(pre_act)).astype(jnp.bfloat16)
        total = total + jnp.dot(d_pre, part[:, :width], preferred_element_type=jnp.float32)
    return total


def taps_by_parity(padded, kernel, flipped):
    rows = padded.shape[1] - 6
    halves = padded.shape[3] - 4
    results = []
    for parity in range(2):
        summed = jnp.zeros((padded.shape[0], rows, halves, padded.shape[4]), jnp.float32)
        for tap_index in range(49):
            row_off = tap_index // 7
            col_off = tap_index % 7 - 3
            if flipped:
                row_off = 6 - row_off
                col_off = -col_off
            first = (parity + col_off) // 2 + 2
            summed = (
                summed
                + padded[:, row_off : row_off + rows, (parity + col_off) % 2, first : first + halves, :]
                * kernel[tap_index]
            )
        results.append(summed)
    return jnp.stack(results, axis=2)


def on_device(
    images,
    kernel_one,
    gain_one,
    shift_one,
    up_one,
    up_bias_one,
    down_one,
    down_bias_one,
    scale_one,
    gain_mid,
    shift_mid,
    merge_weight,
    merge_bias,
    kernel_two,
    gain_two,
    shift_two,
    up_two,
    up_bias_two,
    down_two,
    down_bias_two,
    scale_two,
    grad_out,
):
    micro_count, tile_rows, tile_cols, width_one = images.shape
    width_two = merge_weight.shape[1]
    half_rows = tile_rows // 2
    half_cols = tile_cols // 2
    rows_one = micro_count * tile_rows * tile_cols
    rows_two = micro_count * half_rows * half_cols

    swap = [(0, 1), (1, 0)]
    side = lax.axis_index("sec")
    row_count = lax.axis_size("row")
    col_count = lax.axis_size("col")
    inner = 4 if row_count % 4 == 0 else row_count
    outer = row_count // inner

    def both_halves(own):
        return (own, lax.ppermute(own, "sec", swap))

    def rolled(bias, roll_rows):
        grid = bias.reshape(2, outer, inner, col_count, -1)
        grid = jnp.concatenate([grid, grid], axis=3)
        row_index = lax.axis_index("row")
        start = (0, 0)
        if roll_rows:
            grid = jnp.concatenate([grid, grid], axis=1)
            grid = jnp.concatenate([grid, grid], axis=2)
            start = (row_index // inner, row_index % inner)
        sizes = (1, outer, inner, col_count, grid.shape[4])
        tail = (*start, lax.axis_index("col"), 0)
        return tuple(
            lax.dynamic_slice(grid, (half, *tail), sizes).reshape(-1) for half in (side, 1 - side)
        )

    share_two = up_two.shape[1]
    packed_one = jnp.concatenate([up_one.T, down_one.T], axis=1)
    packed = jnp.concatenate([up_two.T, down_two.T, packed_one], axis=0)
    column = ring_collect(packed[None], "col", col_count, 1)
    part_one = column[:, 2 * share_two :].reshape(-1, 2 * width_one)
    part_two = jnp.concatenate(
        [
            column[:, :share_two].reshape(-1, width_two),
            column[:, share_two : 2 * share_two].reshape(-1, width_two),
        ],
        axis=1,
    )
    own_two = lax.all_gather(part_two, "row", axis=0, tiled=True)
    own_one = ring_collect(ring_collect(part_one, "row", inner, 1), "row", outer, inner)
    pair_one = both_halves(own_one)
    pair_two = both_halves(own_two)
    bias_one = rolled(up_bias_one, True)
    bias_two = rolled(up_bias_two, False)

    images_par = images.reshape(micro_count, tile_rows, half_cols, 2, width_one)
    images_par = images_par.transpose(0, 1, 3, 2, 4)
    rims_one = (("row", 1, 3), ("col", 3, 2))
    rims_two = (("row", 1, 3), ("col", 2, 3))
    conv_one = taps_by_parity(
        with_halo(images_par, rims_one).astype(jnp.float32), kernel_one, False
    ).reshape(rows_one, width_one)
    scaled_one, inv_one, normed_one = norm_forward(conv_one, gain_one, shift_one)
    normed_one = normed_one.astype(jnp.bfloat16)
    branch_one, pre_one = dense_forward(normed_one, pair_one, bias_one, down_bias_one)
    section_out = (
        images_par.reshape(rows_one, width_one).astype(jnp.float32) + scale_one * branch_one
    ).astype(jnp.bfloat16)
    scaled_mid, inv_mid, normed_mid = norm_forward(
        section_out.astype(jnp.float32), gain_mid, shift_mid
    )
    patches = normed_mid.astype(jnp.bfloat16).reshape(
        micro_count * half_rows, 4, half_cols, width_one
    )
    patches = jnp.concatenate(
        [patches[:, place].reshape(rows_two, width_one) for place in range(4)], axis=1
    )
    merged = (
        jnp.dot(patches, merge_weight, preferred_element_type=jnp.float32) + merge_bias
    ).astype(jnp.bfloat16)
    merged_tile = merged.reshape(micro_count, half_rows, half_cols, width_two)
    padded_two = with_halo(merged_tile, rims_two).astype(jnp.float32)
    conv_two = (
        taps_last(padded_two, kernel_two, half_rows, half_cols, False)
        .reshape(rows_two, width_two)
        .astype(jnp.bfloat16)
    )
    scaled_two, inv_two, normed_two = norm_forward(
        conv_two.astype(jnp.float32), gain_two, shift_two
    )
    normed_two = normed_two.astype(jnp.bfloat16)
    branch_two, pre_two = dense_forward(normed_two, pair_two, bias_two, down_bias_two)
    features = (merged.astype(jnp.float32) + scale_two * branch_two).astype(jnp.bfloat16)
    grad_rows = grad_out.reshape(rows_two, width_two)
    d_branch_two = (grad_rows.astype(jnp.float32) * scale_two).astype(jnp.bfloat16)
    d_normed_two = dense_backward(d_branch_two, pre_two, pair_two)
    d_conv_two = norm_backward(d_normed_two, scaled_two, inv_two, gain_two).astype(jnp.bfloat16)
    back_tile = d_conv_two.reshape(micro_count, half_rows, half_cols, width_two)
    padded_back = with_halo(back_tile, rims_two).astype(jnp.float32)
    d_taps = (
        taps_last(padded_back, kernel_two, half_rows, half_cols, True)
        .reshape(rows_two, width_two)
        .astype(jnp.bfloat16)
    )
    d_taps = lax.optimization_barrier(d_taps).astype(jnp.float32)
    d_merged = (d_taps + grad_rows.astype(jnp.float32)).astype(jnp.bfloat16)
    d_patches = contract_last(d_merged, merge_weight)
    d_normed_mid = jnp.stack(
        [
            d_patches[:, place * width_one : (place + 1) * width_one].reshape(
                micro_count * half_rows, half_cols, width_one
            )
            for place in range(4)
        ],
        axis=1,
    ).reshape(rows_one, width_one)
    upstream_one = norm_backward(d_normed_mid, scaled_mid, inv_mid, gain_mid)
    d_branch_one = (upstream_one * scale_one).astype(jnp.bfloat16)
    d_normed_one = dense_backward(d_branch_one, pre_one, pair_one)
    d_conv_one = norm_backward(d_normed_one, scaled_one, inv_one, gain_one).astype(jnp.bfloat16)
    d_conv_one = d_conv_one.reshape(micro_count, tile_rows, 2, half_cols, width_one)
    back_one = taps_by_parity(
        with_halo(d_conv_one, rims_one).astype(jnp.float32), kernel_one, True
    ).reshape(rows_one, width_one)
    input_grad = (back_one + upstream_one).astype(jnp.bfloat16)
    input_grad = input_grad.reshape(micro_count, tile_rows, 2, half_cols, width_one)
    input_grad = input_grad.transpose(0, 1, 3, 2, 4).reshape(images.shape)
    return (features.reshape(micro_count, half_rows, half_cols, width_two), input_grad)


def solution(mesh):
    in_specs = (
        P("sec", "row", "col", None),
        P(),
        P(),
        P(),
        P(None, ("sec", "row", "col")),
        P(),
        P(None, ("sec", "row", "col")),
        P(),
        P(),
        P(),
        P(),
        P(),
        P(),
        P(),
        P(),
        P(),
        P(None, ("sec", "row", "col")),
        P(),
        P(None, ("sec", "row", "col")),
        P(),
        P(),
        P("sec", "row", "col", None),
    )
    out_specs = (P("sec", "row", "col", None), P("sec", "row", "col", None))
    return jax.shard_map(
        on_device, mesh=mesh, in_specs=in_specs, out_specs=out_specs, check_vma=False
    )
```

```python
import jax
import jax.numpy as jnp
from jax import lax
from jax.experimental import pallas as pl
from jax.experimental.pallas import tpu as pltpu
from jax.sharding import PartitionSpec as P

norm_eps = 1e-06


def exchange(block, axis, dim, width):
    count = lax.axis_size(axis)
    forward = [(i, i + 1) for i in range(count - 1)]
    backward = [(target, source) for source, target in forward]
    low = lax.ppermute(
        lax.slice_in_dim(block, block.shape[dim] - width, None, axis=dim), axis, forward
    )
    high = lax.ppermute(lax.slice_in_dim(block, 0, width, axis=dim), axis, backward)
    return low, high


def halo_of(block, width):
    dim = block.ndim - 2
    top, bottom = exchange(block, "row", 0, 3)

    def edge(first, last):
        parts = [lax.slice_in_dim(part, first, last, axis=dim) for part in (top, block, bottom)]
        return jnp.concatenate(parts, axis=0)

    count = lax.axis_size("col")
    extent = block.shape[dim]
    forward = [(i, i + 1) for i in range(count - 1)]
    backward = [(target, source) for source, target in forward]
    left = lax.ppermute(edge(extent - width, extent), "col", forward)
    right = lax.ppermute(edge(0, width), "col", backward)
    return top, bottom, left, right


def ring_collect(piece, axis, inner, stride):
    count = lax.axis_size(axis)
    found = [piece]
    for shift in range(1, inner):
        pairs = []
        for target in range(count):
            place = (target // stride) % inner
            source = target + ((place + shift) % inner - place) * stride
            pairs.append((source, target))
        found.append(lax.ppermute(piece, axis, pairs))
    return jnp.concatenate(found, axis=0)


def gelu_exact(values):
    return 0.5 * values * (1.0 + lax.erf(values * 0.7071067811865476))


def gelu_slope(values):
    return (
        0.5 * (1.0 + lax.erf(values * 0.7071067811865476))
        + values * jnp.exp(-0.5 * values * values) * 0.3989422804014327
    )


def norm_forward(values, norm_gain, norm_shift):
    center = values - jnp.mean(values, axis=-1, keepdims=True)
    inv_std = lax.rsqrt(jnp.mean(center * center, axis=-1, keepdims=True) + norm_eps)
    scaled = center * inv_std
    return (scaled, inv_std, scaled * norm_gain + norm_shift)


def norm_backward(upstream, scaled, inv_std, norm_gain):
    weighted = upstream * norm_gain
    mean_one = jnp.mean(weighted, axis=-1, keepdims=True)
    mean_two = jnp.mean(weighted * scaled, axis=-1, keepdims=True)
    return inv_std * (weighted - mean_one - scaled * mean_two)


def contract_last(left_side, right_side):
    return lax.dot_general(
        left_side, right_side, (((1,), (1,)), ((), ())), preferred_element_type=jnp.float32
    )


def dense_forward(normed, weights, up_bias, down_bias):
    width = normed.shape[1]
    pre_acts = []
    branch = down_bias
    for part, part_bias in zip(weights, up_bias):
        pre_act = contract_last(normed, part[:, :width]) + part_bias
        hidden = gelu_exact(pre_act).astype(jnp.bfloat16)
        branch = branch + jnp.dot(hidden, part[:, width:], preferred_element_type=jnp.float32)
        pre_acts.append(pre_act)
    return (branch, pre_acts)


def dense_backward(d_branch, pre_acts, weights):
    width = d_branch.shape[1]
    total = 0.0
    for part, pre_act in zip(weights, pre_acts):
        d_hidden = contract_last(d_branch, part[:, width:])
        d_pre = (d_hidden * gelu_slope(pre_act)).astype(jnp.bfloat16)
        total = total + jnp.dot(d_pre, part[:, :width], preferred_element_type=jnp.float32)
    return total


lanes = 128


def fill_rows(frame, source, first, width):
    for row in range(source.shape[0]):
        for tile in range(source.shape[-1] // lanes):
            part = source[row, :, tile * lanes : (tile + 1) * lanes].astype(jnp.float32)
            frame[tile, first + row, 8 : 8 + width, :] = part


def fill_edges(frame, left, right, width):
    for row in range(left.shape[0]):
        for tile in range(left.shape[-1] // lanes):
            span = slice(tile * lanes, (tile + 1) * lanes)
            frame[tile, row, 5:8, :] = left[row, :, span].astype(jnp.float32)
            frame[tile, row, 8 + width : 11 + width, :] = right[row, :, span].astype(jnp.float32)


def fill_parity_rows(frame, source, first):
    halves = source.shape[2]
    for row in range(source.shape[0]):
        for tile in range(source.shape[-1] // lanes):
            for parity in range(2):
                part = source[row, parity, :, tile * lanes : (tile + 1) * lanes]
                frame[tile, first + row, pl.ds(8 + parity, halves, stride=2), :] = part.astype(
                    jnp.float32
                )


def fill_parity_edges(frame, left, right, width):
    for row in range(left.shape[0]):
        for tile in range(left.shape[-1] // lanes):
            span = slice(tile * lanes, (tile + 1) * lanes)
            for parity in range(2):
                for half in range(2):
                    col = 2 * half + parity
                    frame[tile, row, 4 + col : 5 + col, :] = left[
                        row, parity, half : half + 1, span
                    ].astype(jnp.float32)
                    frame[tile, row, 8 + width + col : 9 + width + col, :] = right[
                        row, parity, half : half + 1, span
                    ].astype(jnp.float32)


def depthwise(frame, taps, tile, rows, cols, first, stride, flipped):
    sums = [jnp.zeros((cols, lanes), jnp.float32) for _ in range(rows)]
    span = pl.ds(pl.multiple_of(tile * lanes, lanes), lanes)
    for tap_col in range(7):
        weights = [taps[pl.ds(7 * tap_row + tap_col, 1), span] for tap_row in range(7)]
        start = 5 + first + (6 - tap_col if flipped else tap_col)
        for row in range(rows + 6):
            if stride == 1:
                values = frame[tile, row, pl.ds(start, cols), :]
            else:
                values = frame[tile, row, pl.ds(start, cols, stride=stride), :]
            for tap_row in range(7):
                target = row - (6 - tap_row if flipped else tap_row)
                if 0 <= target < rows:
                    sums[target] = sums[target] + values * weights[tap_row]
    return sums


def norm_rows(values_ref, normed_ref, gain_ref, shift_ref, chunk):
    gain = gain_ref[...]
    shift = shift_ref[...]

    def step(index, carry):
        span = pl.ds(pl.multiple_of(index * chunk, chunk), chunk)
        values = values_ref[span, :].astype(jnp.float32)
        normed_ref[span, :] = norm_forward(values, gain, shift)[2].astype(normed_ref.dtype)
        return carry

    lax.fori_loop(0, values_ref.shape[0] // chunk, step, 0)


def conv_one_kernel(
    tile_ref, top, bottom, left, right, taps, gain, shift, normed, conv, residual, frame
):
    rows, width, channels = tile_ref.shape
    halves = width // 2
    fill_rows(frame, top, 0, width)
    fill_rows(frame, tile_ref, 3, width)
    fill_rows(frame, bottom, 3 + rows, width)
    fill_edges(frame, left, right, width)

    def step(tile, carry):
        span = pl.ds(pl.multiple_of(tile * lanes, lanes), lanes)
        for parity in range(2):
            sums = depthwise(frame, taps, tile, rows, halves, parity, 2, False)
            for row in range(rows):
                place = pl.ds(row * width + parity * halves, halves)
                conv[place, span] = sums[row]
                own = frame[tile, 3 + row, pl.ds(8 + parity, halves, stride=2), :]
                residual[place, span] = own.astype(residual.dtype)
        return carry

    lax.fori_loop(0, channels // lanes, step, 0)
    norm_rows(conv, normed, gain, shift, 64)


def back_one_kernel(tile_ref, top, bottom, left, right, taps, upstream, out, frame, total):
    rows, _, halves, channels = tile_ref.shape
    width = 2 * halves
    fill_parity_rows(frame, top, 0)
    fill_parity_rows(frame, tile_ref, 3)
    fill_parity_rows(frame, bottom, 3 + rows)
    fill_parity_edges(frame, left, right, width)

    def step(tile, carry):
        span = pl.ds(pl.multiple_of(tile * lanes, lanes), lanes)
        for parity in range(2):
            sums = depthwise(frame, taps, tile, rows, halves, parity, 2, True)
            for row in range(rows):
                place = pl.ds(row * width + parity * halves, halves)
                total[row, pl.ds(parity, halves, stride=2), :] = sums[row] + upstream[place, span]
        for row in range(rows):
            out[row, :, span] = total[row].astype(out.dtype)
        return carry

    lax.fori_loop(0, channels // lanes, step, 0)


def conv_two_kernel(tile_ref, top, bottom, left, right, taps, gain, shift, normed, conv, frame):
    rows, width, channels = tile_ref.shape
    fill_rows(frame, top, 0, width)
    fill_rows(frame, tile_ref, 3, width)
    fill_rows(frame, bottom, 3 + rows, width)
    fill_edges(frame, left, right, width)

    def step(tile, carry):
        span = pl.ds(pl.multiple_of(tile * lanes, lanes), lanes)
        sums = depthwise(frame, taps, tile, rows, width, 0, 1, False)
        for row in range(rows):
            conv[pl.ds(row * width, width), span] = sums[row].astype(conv.dtype)
        return carry

    lax.fori_loop(0, channels // lanes, step, 0)
    norm_rows(conv, normed, gain, shift, 64)


def back_two_kernel(tile_ref, top, bottom, left, right, taps, grad, out, frame):
    rows, width, channels = tile_ref.shape
    fill_rows(frame, top, 0, width)
    fill_rows(frame, tile_ref, 3, width)
    fill_rows(frame, bottom, 3 + rows, width)
    fill_edges(frame, left, right, width)

    def step(tile, carry):
        span = pl.ds(pl.multiple_of(tile * lanes, lanes), lanes)
        sums = depthwise(frame, taps, tile, rows, width, 0, 1, True)
        for row in range(rows):
            place = pl.ds(row * width, width)
            d_taps = sums[row].astype(jnp.bfloat16).astype(jnp.float32)
            out[place, span] = (d_taps + grad[place, span].astype(jnp.float32)).astype(out.dtype)
        return carry

    lax.fori_loop(0, channels // lanes, step, 0)


def tile_call(kernel, outputs, rows, width, channels, operands, extra=()):
    whole = pl.BlockSpec(memory_space=pltpu.VMEM)
    frame = pltpu.VMEM((channels // lanes, rows + 6, width + 16, lanes), jnp.float32)
    return pl.pallas_call(
        kernel,
        out_shape=outputs,
        in_specs=[whole] * len(operands),
        out_specs=jax.tree.map(lambda _: whole, outputs),
        scratch_shapes=[frame, *extra],
        compiler_params=pltpu.CompilerParams(vmem_limit_bytes=32 * 1024 * 1024),
    )(*operands)


def on_device(
    images,
    kernel_one,
    gain_one,
    shift_one,
    up_one,
    up_bias_one,
    down_one,
    down_bias_one,
    scale_one,
    gain_mid,
    shift_mid,
    merge_weight,
    merge_bias,
    kernel_two,
    gain_two,
    shift_two,
    up_two,
    up_bias_two,
    down_two,
    down_bias_two,
    scale_two,
    grad_out,
):
    micro_count, tile_rows, tile_cols, width_one = images.shape
    width_two = merge_weight.shape[1]
    half_rows = tile_rows // 2
    half_cols = tile_cols // 2
    rows_one = micro_count * tile_rows * tile_cols
    rows_two = micro_count * half_rows * half_cols

    swap = [(0, 1), (1, 0)]
    side = lax.axis_index("sec")
    row_count = lax.axis_size("row")
    col_count = lax.axis_size("col")
    inner = 4 if row_count % 4 == 0 else row_count
    outer = row_count // inner

    def both_halves(own):
        return (own, lax.ppermute(own, "sec", swap))

    def rolled(bias, roll_rows):
        grid = bias.reshape(2, outer, inner, col_count, -1)
        grid = jnp.concatenate([grid, grid], axis=3)
        row_index = lax.axis_index("row")
        start = (0, 0)
        if roll_rows:
            grid = jnp.concatenate([grid, grid], axis=1)
            grid = jnp.concatenate([grid, grid], axis=2)
            start = (row_index // inner, row_index % inner)
        sizes = (1, outer, inner, col_count, grid.shape[4])
        tail = (*start, lax.axis_index("col"), 0)
        return tuple(
            lax.dynamic_slice(grid, (half, *tail), sizes).reshape(-1) for half in (side, 1 - side)
        )

    share_two = up_two.shape[1]
    packed_one = jnp.concatenate([up_one.T, down_one.T], axis=1)
    packed = jnp.concatenate([up_two.T, down_two.T, packed_one], axis=0)
    column = ring_collect(packed[None], "col", col_count, 1)
    part_one = column[:, 2 * share_two :].reshape(-1, 2 * width_one)
    part_two = jnp.concatenate(
        [
            column[:, :share_two].reshape(-1, width_two),
            column[:, share_two : 2 * share_two].reshape(-1, width_two),
        ],
        axis=1,
    )
    own_two = lax.all_gather(part_two, "row", axis=0, tiled=True)
    own_one = ring_collect(ring_collect(part_one, "row", inner, 1), "row", outer, inner)
    pair_one = both_halves(own_one)
    pair_two = both_halves(own_two)
    bias_one = rolled(up_bias_one, True)
    bias_two = rolled(up_bias_two, False)

    image_tile = images.reshape(tile_rows, tile_cols, width_one)
    normed_one, conv_one, images_par = tile_call(
        conv_one_kernel,
        (
            jax.ShapeDtypeStruct((rows_one, width_one), jnp.bfloat16),
            jax.ShapeDtypeStruct((rows_one, width_one), jnp.float32),
            jax.ShapeDtypeStruct((rows_one, width_one), jnp.bfloat16),
        ),
        tile_rows,
        tile_cols,
        width_one,
        (image_tile, *halo_of(image_tile, 3), kernel_one, gain_one[None], shift_one[None]),
    )
    scaled_one, inv_one, _ = norm_forward(conv_one, gain_one, shift_one)
    branch_one, pre_one = dense_forward(normed_one, pair_one, bias_one, down_bias_one)
    section_out = (
        images_par.astype(jnp.float32) + scale_one * branch_one
    ).astype(jnp.bfloat16)
    scaled_mid, inv_mid, normed_mid = norm_forward(
        section_out.astype(jnp.float32), gain_mid, shift_mid
    )
    patches = normed_mid.astype(jnp.bfloat16).reshape(
        micro_count * half_rows, 4, half_cols, width_one
    )
    patches = jnp.concatenate(
        [patches[:, place].reshape(rows_two, width_one) for place in range(4)], axis=1
    )
    merged = (
        jnp.dot(patches, merge_weight, preferred_element_type=jnp.float32) + merge_bias
    ).astype(jnp.bfloat16)
    merged_tile = merged.reshape(half_rows, half_cols, width_two)
    normed_two, conv_two = tile_call(
        conv_two_kernel,
        (
            jax.ShapeDtypeStruct((rows_two, width_two), jnp.bfloat16),
            jax.ShapeDtypeStruct((rows_two, width_two), jnp.bfloat16),
        ),
        half_rows,
        half_cols,
        width_two,
        (merged_tile, *halo_of(merged_tile, 3), kernel_two, gain_two[None], shift_two[None]),
    )
    scaled_two, inv_two, _ = norm_forward(conv_two.astype(jnp.float32), gain_two, shift_two)
    branch_two, pre_two = dense_forward(normed_two, pair_two, bias_two, down_bias_two)
    features = (merged.astype(jnp.float32) + scale_two * branch_two).astype(jnp.bfloat16)
    grad_rows = grad_out.reshape(rows_two, width_two)
    d_branch_two = (grad_rows.astype(jnp.float32) * scale_two).astype(jnp.bfloat16)
    d_normed_two = dense_backward(d_branch_two, pre_two, pair_two)
    d_conv_two = norm_backward(d_normed_two, scaled_two, inv_two, gain_two).astype(jnp.bfloat16)
    back_tile = d_conv_two.reshape(half_rows, half_cols, width_two)
    d_merged = tile_call(
        back_two_kernel,
        jax.ShapeDtypeStruct((rows_two, width_two), jnp.bfloat16),
        half_rows,
        half_cols,
        width_two,
        (back_tile, *halo_of(back_tile, 3), kernel_two, grad_rows),
    )
    d_patches = contract_last(d_merged, merge_weight)
    d_normed_mid = jnp.stack(
        [
            d_patches[:, place * width_one : (place + 1) * width_one].reshape(
                micro_count * half_rows, half_cols, width_one
            )
            for place in range(4)
        ],
        axis=1,
    ).reshape(rows_one, width_one)
    upstream_one = norm_backward(d_normed_mid, scaled_mid, inv_mid, gain_mid)
    d_branch_one = (upstream_one * scale_one).astype(jnp.bfloat16)
    d_normed_one = dense_backward(d_branch_one, pre_one, pair_one)
    d_conv_one = norm_backward(d_normed_one, scaled_one, inv_one, gain_one).astype(jnp.bfloat16)
    d_conv_one = d_conv_one.reshape(tile_rows, 2, half_cols, width_one)
    input_grad = tile_call(
        back_one_kernel,
        jax.ShapeDtypeStruct((tile_rows, tile_cols, width_one), jnp.bfloat16),
        tile_rows,
        tile_cols,
        width_one,
        (d_conv_one, *halo_of(d_conv_one, 2), kernel_one, upstream_one),
        (pltpu.VMEM((tile_rows, tile_cols, lanes), jnp.float32),),
    ).reshape(images.shape)
    return (features.reshape(micro_count, half_rows, half_cols, width_two), input_grad)


def solution(mesh):
    in_specs = (
        P("sec", "row", "col", None),
        P(),
        P(),
        P(),
        P(None, ("sec", "row", "col")),
        P(),
        P(None, ("sec", "row", "col")),
        P(),
        P(),
        P(),
        P(),
        P(),
        P(),
        P(),
        P(),
        P(),
        P(None, ("sec", "row", "col")),
        P(),
        P(None, ("sec", "row", "col")),
        P(),
        P(),
        P("sec", "row", "col", None),
    )
    out_specs = (P("sec", "row", "col", None), P("sec", "row", "col", None))
    return jax.shard_map(
        on_device, mesh=mesh, in_specs=in_specs, out_specs=out_specs, check_vma=False
    )
```

```python
import jax
import jax.numpy as jnp
from jax import lax
from jax.experimental import pallas as pl
from jax.experimental.pallas import tpu as pltpu
from jax.sharding import PartitionSpec as P

norm_eps = 1e-06


def exchange(block, axis, dim, width):
    count = lax.axis_size(axis)
    forward = [(i, i + 1) for i in range(count - 1)]
    backward = [(target, source) for source, target in forward]
    low = lax.ppermute(
        lax.slice_in_dim(block, block.shape[dim] - width, None, axis=dim), axis, forward
    )
    high = lax.ppermute(lax.slice_in_dim(block, 0, width, axis=dim), axis, backward)
    return low, high


def halo_of(block, width):
    dim = block.ndim - 2
    top, bottom = exchange(block, "row", 0, 3)

    def edge(first, last):
        parts = [lax.slice_in_dim(part, first, last, axis=dim) for part in (top, block, bottom)]
        return jnp.concatenate(parts, axis=0)

    count = lax.axis_size("col")
    extent = block.shape[dim]
    forward = [(i, i + 1) for i in range(count - 1)]
    backward = [(target, source) for source, target in forward]
    left = lax.ppermute(edge(extent - width, extent), "col", forward)
    right = lax.ppermute(edge(0, width), "col", backward)
    return top, bottom, left, right


def ring_collect(piece, axis, inner, stride):
    count = lax.axis_size(axis)
    own_place = (lax.axis_index(axis) // stride) % inner
    found = jnp.zeros((inner, *piece.shape), piece.dtype)
    found = lax.dynamic_update_index_in_dim(found, piece, own_place, 0)
    for shift in range(1, inner):
        pairs = []
        for target in range(count):
            place = (target // stride) % inner
            source = target + ((place + shift) % inner - place) * stride
            pairs.append((source, target))
        arrived = lax.ppermute(piece, axis, pairs)
        found = lax.dynamic_update_index_in_dim(found, arrived, (own_place + shift) % inner, 0)
    return found


def normal_cdf(values):
    return 0.5 * (1.0 + lax.erf(values * 0.7071067811865476))


def slope_from(values, cdf):
    return cdf + values * jnp.exp(-0.5 * values * values) * 0.3989422804014327


def norm_forward(values, norm_gain, norm_shift):
    center = values - jnp.mean(values, axis=-1, keepdims=True)
    inv_std = lax.rsqrt(jnp.mean(center * center, axis=-1, keepdims=True) + norm_eps)
    scaled = center * inv_std
    return (scaled, inv_std, scaled * norm_gain + norm_shift)


def norm_backward(upstream, scaled, inv_std, norm_gain):
    weighted = upstream * norm_gain
    mean_one = jnp.mean(weighted, axis=-1, keepdims=True)
    mean_two = jnp.mean(weighted * scaled, axis=-1, keepdims=True)
    return inv_std * (weighted - mean_one - scaled * mean_two)


def contract_last(left_side, right_side):
    return lax.dot_general(
        left_side, right_side, (((1,), (1,)), ((), ())), preferred_element_type=jnp.float32
    )


lanes = 128


def fill_rows(frame, source, first, width):
    for row in range(source.shape[0]):
        for tile in range(source.shape[-1] // lanes):
            part = source[row, :, tile * lanes : (tile + 1) * lanes].astype(jnp.float32)
            frame[tile, first + row, 8 : 8 + width, :] = part


def fill_edges(frame, left, right, width):
    for row in range(left.shape[0]):
        for tile in range(left.shape[-1] // lanes):
            span = slice(tile * lanes, (tile + 1) * lanes)
            frame[tile, row, 5:8, :] = left[row, :, span].astype(jnp.float32)
            frame[tile, row, 8 + width : 11 + width, :] = right[row, :, span].astype(jnp.float32)


def fill_parity_rows(frame, source, first):
    halves = source.shape[2]
    for row in range(source.shape[0]):
        for tile in range(source.shape[-1] // lanes):
            for parity in range(2):
                part = source[row, parity, :, tile * lanes : (tile + 1) * lanes]
                frame[tile, first + row, pl.ds(8 + parity, halves, stride=2), :] = part.astype(
                    jnp.float32
                )


def fill_parity_edges(frame, left, right, width):
    for row in range(left.shape[0]):
        for tile in range(left.shape[-1] // lanes):
            span = slice(tile * lanes, (tile + 1) * lanes)
            for parity in range(2):
                for half in range(2):
                    col = 2 * half + parity
                    frame[tile, row, 4 + col : 5 + col, :] = left[
                        row, parity, half : half + 1, span
                    ].astype(jnp.float32)
                    frame[tile, row, 8 + width + col : 9 + width + col, :] = right[
                        row, parity, half : half + 1, span
                    ].astype(jnp.float32)


def depthwise(frame, taps, tile, rows, cols, first, stride, flipped):
    sums = [jnp.zeros((cols, lanes), jnp.float32) for _ in range(rows)]
    span = pl.ds(pl.multiple_of(tile * lanes, lanes), lanes)
    for tap_col in range(7):
        weights = [taps[pl.ds(7 * tap_row + tap_col, 1), span] for tap_row in range(7)]
        start = 5 + first + (6 - tap_col if flipped else tap_col)
        for row in range(rows + 6):
            if stride == 1:
                values = frame[tile, row, pl.ds(start, cols), :]
            else:
                values = frame[tile, row, pl.ds(start, cols, stride=stride), :]
            for tap_row in range(7):
                target = row - (6 - tap_row if flipped else tap_row)
                if 0 <= target < rows:
                    sums[target] = sums[target] + values * weights[tap_row]
    return sums


def norm_rows(values_ref, normed_ref, gain_ref, shift_ref, chunk):
    gain = gain_ref[...]
    shift = shift_ref[...]

    def step(index, carry):
        span = pl.ds(pl.multiple_of(index * chunk, chunk), chunk)
        values = values_ref[span, :].astype(jnp.float32)
        normed_ref[span, :] = norm_forward(values, gain, shift)[2].astype(normed_ref.dtype)
        return carry

    lax.fori_loop(0, values_ref.shape[0] // chunk, step, 0)


def conv_one_kernel(
    tile_ref, top, bottom, left, right, taps, gain, shift, normed, conv, residual, frame
):
    rows, width, channels = tile_ref.shape
    halves = width // 2
    fill_rows(frame, top, 0, width)
    fill_rows(frame, tile_ref, 3, width)
    fill_rows(frame, bottom, 3 + rows, width)
    fill_edges(frame, left, right, width)

    def step(tile, carry):
        span = pl.ds(pl.multiple_of(tile * lanes, lanes), lanes)
        for parity in range(2):
            sums = depthwise(frame, taps, tile, rows, halves, parity, 2, False)
            for row in range(rows):
                place = pl.ds(row * width + parity * halves, halves)
                conv[place, span] = sums[row]
                own = frame[tile, 3 + row, pl.ds(8 + parity, halves, stride=2), :]
                residual[place, span] = own.astype(residual.dtype)
        return carry

    lax.fori_loop(0, channels // lanes, step, 0)
    norm_rows(conv, normed, gain, shift, 64)


def back_one_kernel(tile_ref, top, bottom, left, right, taps, upstream, out, frame, total):
    rows, _, halves, channels = tile_ref.shape
    width = 2 * halves
    fill_parity_rows(frame, top, 0)
    fill_parity_rows(frame, tile_ref, 3)
    fill_parity_rows(frame, bottom, 3 + rows)
    fill_parity_edges(frame, left, right, width)

    def step(tile, carry):
        span = pl.ds(pl.multiple_of(tile * lanes, lanes), lanes)
        for parity in range(2):
            sums = depthwise(frame, taps, tile, rows, halves, parity, 2, True)
            for row in range(rows):
                place = pl.ds(row * width + parity * halves, halves)
                total[row, pl.ds(parity, halves, stride=2), :] = sums[row] + upstream[place, span]
        for row in range(rows):
            out[row, :, span] = total[row].astype(out.dtype)
        return carry

    lax.fori_loop(0, channels // lanes, step, 0)


def conv_two_kernel(tile_ref, top, bottom, left, right, taps, gain, shift, normed, conv, frame):
    rows, width, channels = tile_ref.shape
    fill_rows(frame, top, 0, width)
    fill_rows(frame, tile_ref, 3, width)
    fill_rows(frame, bottom, 3 + rows, width)
    fill_edges(frame, left, right, width)

    def step(tile, carry):
        span = pl.ds(pl.multiple_of(tile * lanes, lanes), lanes)
        sums = depthwise(frame, taps, tile, rows, width, 0, 1, False)
        for row in range(rows):
            conv[pl.ds(row * width, width), span] = sums[row].astype(conv.dtype)
        return carry

    lax.fori_loop(0, channels // lanes, step, 0)
    norm_rows(conv, normed, gain, shift, 64)


def back_two_kernel(tile_ref, top, bottom, left, right, taps, grad, out, frame):
    rows, width, channels = tile_ref.shape
    fill_rows(frame, top, 0, width)
    fill_rows(frame, tile_ref, 3, width)
    fill_rows(frame, bottom, 3 + rows, width)
    fill_edges(frame, left, right, width)

    def step(tile, carry):
        span = pl.ds(pl.multiple_of(tile * lanes, lanes), lanes)
        sums = depthwise(frame, taps, tile, rows, width, 0, 1, True)
        for row in range(rows):
            place = pl.ds(row * width, width)
            d_taps = sums[row].astype(jnp.bfloat16).astype(jnp.float32)
            out[place, span] = (d_taps + grad[place, span].astype(jnp.float32)).astype(out.dtype)
        return carry

    lax.fori_loop(0, channels // lanes, step, 0)


def dot(left_side, right_side):
    return jnp.dot(left_side, right_side, preferred_element_type=jnp.float32)


def row_blocks(total, size):
    size = min(total, size)
    return [slice(first, first + size) for first in range(0, total, size)]


def mlp_one_half(normed, weights, bias, branch):
    width = normed.shape[1]

    @pl.when(pl.program_id(0) == 0)
    def _():
        branch[...] = jnp.zeros_like(branch)

    for rows in row_blocks(normed.shape[0], 256):
        pre_act = contract_last(normed[rows, :], weights[:, :width]) + bias[...]
        hidden = (pre_act * normal_cdf(pre_act)).astype(jnp.bfloat16)
        branch[rows, :] += dot(hidden, weights[:, width:])


def mlp_one_finish(
    normed, weights, bias, partial, residual, down_bias, scale, gain, shift, merge, merge_bias,
    section, merged, branch, patches,
):
    mlp_one_half(normed, weights, bias, branch)
    positions, width = normed.shape
    quarter = patches.shape[0]
    half_cols = patches.shape[2]

    @pl.when(pl.program_id(0) == pl.num_programs(0) - 1)
    def _():
        step_rows = 4 * half_cols

        def step(index, carry):
            rows = pl.ds(pl.multiple_of(index * step_rows, step_rows), step_rows)
            total = branch[rows, :] + partial[rows, :] + down_bias[...]
            out = (residual[rows, :].astype(jnp.float32) + scale[...] * total).astype(jnp.bfloat16)
            section[rows, :] = out
            normal = norm_forward(out.astype(jnp.float32), gain[...], shift[...])[2]
            normal = normal.astype(jnp.bfloat16)
            for place in range(4):
                patches[index, place] = normal[place * half_cols : (place + 1) * half_cols, :]
            return carry

        lax.fori_loop(0, quarter, step, 0)
        total = merge_bias[...]
        for place in range(4):
            patch = patches[:, place].reshape(quarter * half_cols, width)
            total = total + dot(patch, merge[place * width : (place + 1) * width, :])
        merged[...] = total.astype(merged.dtype)


def slope_one_kernel(normed, own, other, bias_own, bias_other, slope_own, slope_other):
    width = normed.shape[1]
    for rows in row_blocks(normed.shape[0], 256):
        for weights, bias, slope in (
            (own, bias_own, slope_own),
            (other, bias_other, slope_other),
        ):
            pre_act = contract_last(normed[rows, :], weights[:, :width]) + bias[...]
            slope[rows, :] = slope_from(pre_act, normal_cdf(pre_act)).astype(slope.dtype)


def back_mlp_one(
    d_merged, merge, section, gain_mid, scale, own, other, slope_own, slope_other, conv, gain,
    d_conv, upstream, d_branch, d_normed,
):
    width = section.shape[1]
    quarter = d_merged.shape[0]
    half_cols = 16
    groups = quarter // half_cols

    @pl.when(pl.program_id(0) == 0)
    def _():
        d_normed[...] = jnp.zeros_like(d_normed)
        for place in range(4):
            d_normal = contract_last(d_merged[...], merge[place * width : (place + 1) * width, :])
            for group in range(groups):
                first = (4 * group + place) * half_cols
                rows = slice(first, first + half_cols)
                values = section[rows, :].astype(jnp.float32)
                scaled, inv_std, _ = norm_forward(values, 1.0, 0.0)
                flow = norm_backward(
                    d_normal[group * half_cols : (group + 1) * half_cols],
                    scaled,
                    inv_std,
                    gain_mid[...],
                )
                upstream[rows, :] = flow
                d_branch[rows, :] = (flow * scale[...]).astype(d_branch.dtype)

    for rows in row_blocks(section.shape[0], 256):
        total = d_normed[rows, :]
        for weights, slope in ((own, slope_own), (other, slope_other)):
            d_hidden = contract_last(d_branch[rows, :], weights[:, width:])
            d_pre = (d_hidden * slope[rows, :].astype(jnp.float32)).astype(jnp.bfloat16)
            total = total + dot(d_pre, weights[:, :width])
        d_normed[rows, :] = total

    @pl.when(pl.program_id(0) == pl.num_programs(0) - 1)
    def _():
        norm_back_rows(conv, d_normed, gain, d_conv, 64)


def norm_back_rows(conv, d_normed, gain, d_conv, chunk):
    def step(index, carry):
        rows = pl.ds(pl.multiple_of(index * chunk, chunk), chunk)
        scaled, inv_std, _ = norm_forward(conv[rows, :].astype(jnp.float32), 1.0, 0.0)
        flow = norm_backward(d_normed[rows, :], scaled, inv_std, gain[...])
        d_conv[rows, :] = flow.astype(d_conv.dtype)
        return carry

    lax.fori_loop(0, conv.shape[0] // chunk, step, 0)


def mlp_two_half(normed, grad, scale, weights, bias, branch, d_normed, d_branch):
    width = normed.shape[1]

    @pl.when(pl.program_id(0) == 0)
    def _():
        branch[...] = jnp.zeros_like(branch)
        d_normed[...] = jnp.zeros_like(d_normed)
        d_branch[...] = (grad[...].astype(jnp.float32) * scale[...]).astype(d_branch.dtype)

    up = weights[:, :width]
    down = weights[:, width:]
    pre_act = contract_last(normed[...], up) + bias[...]
    d_hidden = contract_last(d_branch[...], down)
    cdf = normal_cdf(pre_act)
    hidden = (pre_act * cdf).astype(jnp.bfloat16)
    d_pre = (d_hidden * slope_from(pre_act, cdf)).astype(jnp.bfloat16)
    branch[...] += dot(hidden, down)
    d_normed[...] += dot(d_pre, up)


def mlp_two_finish(
    normed, grad, scale, weights, bias, partial, d_partial, merged, down_bias, conv, gain,
    features, d_conv, branch, d_normed, d_branch,
):
    mlp_two_half(normed, grad, scale, weights, bias, branch, d_normed, d_branch)

    @pl.when(pl.program_id(0) == pl.num_programs(0) - 1)
    def _():
        total = branch[...] + partial[...] + down_bias[...]
        out = merged[...].astype(jnp.float32) + scale[...] * total
        features[...] = out.astype(features.dtype)
        d_normed[...] += d_partial[...]
        norm_back_rows(conv, d_normed, gain, d_conv, 64)


megabyte = 1024 * 1024


def shape_of(dims, dtype):
    return jax.ShapeDtypeStruct(dims, dtype)


def block_call(kernel, outputs, operands, scratch, steps=1, split=(), limit=40):
    def spec_of(array, key):
        dims = list(array.shape)
        axis = dict(split).get(key)
        if axis is not None:
            dims[axis] //= steps

        def index_map(step):
            return tuple(step if place == axis else 0 for place in range(len(dims)))

        return pl.BlockSpec(tuple(dims), index_map)

    return pl.pallas_call(
        kernel,
        grid=(steps,),
        out_shape=outputs,
        in_specs=[spec_of(array, index) for index, array in enumerate(operands)],
        out_specs=[spec_of(array, "out%d" % index) for index, array in enumerate(outputs)],
        scratch_shapes=scratch,
        compiler_params=pltpu.CompilerParams(vmem_limit_bytes=limit * megabyte),
    )(*operands)


def tile_call(kernel, outputs, rows, width, channels, operands, extra=()):
    frame = pltpu.VMEM((channels // lanes, rows + 6, width + 16, lanes), jnp.float32)
    return block_call(kernel, outputs, operands, [frame, *extra])


def on_device(
    images,
    kernel_one,
    gain_one,
    shift_one,
    up_one,
    up_bias_one,
    down_one,
    down_bias_one,
    scale_one,
    gain_mid,
    shift_mid,
    merge_weight,
    merge_bias,
    kernel_two,
    gain_two,
    shift_two,
    up_two,
    up_bias_two,
    down_two,
    down_bias_two,
    scale_two,
    grad_out,
):
    micro_count, tile_rows, tile_cols, width_one = images.shape
    width_two = merge_weight.shape[1]
    half_rows = tile_rows // 2
    half_cols = tile_cols // 2
    rows_one = micro_count * tile_rows * tile_cols
    rows_two = micro_count * half_rows * half_cols

    swap = [(0, 1), (1, 0)]
    side = lax.axis_index("sec")
    row_count = lax.axis_size("row")
    col_count = lax.axis_size("col")
    inner = 4 if row_count % 4 == 0 else row_count
    outer = row_count // inner
    bfloat = jnp.bfloat16

    def bias_halves(bias):
        halves = bias.reshape(2, 1, -1)
        return (
            jnp.where(side == 0, halves[0], halves[1]),
            jnp.where(side == 0, halves[1], halves[0]),
        )

    share_two = up_two.shape[1]
    packed_one = jnp.concatenate([up_one.T, down_one.T], axis=1)
    packed = jnp.concatenate([up_two.T, down_two.T, packed_one], axis=0)
    column = ring_collect(packed, "col", col_count, 1)
    part_one = column[:, 2 * share_two :].reshape(-1, 2 * width_one)
    part_two = jnp.concatenate(
        [
            column[:, :share_two].reshape(-1, width_two),
            column[:, share_two : 2 * share_two].reshape(-1, width_two),
        ],
        axis=1,
    )
    own_two = lax.all_gather(part_two, "row", axis=0, tiled=True)
    own_one = ring_collect(part_one, "row", inner, 1).reshape(-1, 2 * width_one)
    own_one = ring_collect(own_one, "row", outer, inner).reshape(-1, 2 * width_one)
    bias_one = bias_halves(up_bias_one)
    bias_two = bias_halves(up_bias_two)

    image_tile = images.reshape(tile_rows, tile_cols, width_one)
    normed_one, conv_one, images_par = tile_call(
        conv_one_kernel,
        (
            shape_of((rows_one, width_one), bfloat),
            shape_of((rows_one, width_one), jnp.float32),
            shape_of((rows_one, width_one), bfloat),
        ),
        tile_rows,
        tile_cols,
        width_one,
        (image_tile, *halo_of(image_tile, 3), kernel_one, gain_one[None], shift_one[None]),
    )
    own_one, normed_one, images_par, bias_one, bias_two = lax.optimization_barrier(
        (own_one, normed_one, images_par, bias_one, bias_two)
    )
    other_one = lax.ppermute(own_one, "sec", swap)
    other_two = lax.ppermute(own_two, "sec", swap)
    steps_one = max(1, own_one.shape[0] // 256)
    steps_two = max(1, own_two.shape[0] // 256)

    (partial_one,) = block_call(
        mlp_one_half,
        (shape_of((rows_one, width_one), jnp.float32),),
        (normed_one, own_one, bias_one[0]),
        [],
        steps_one,
        ((1, 0), (2, 1)),
    )
    section_out, merged = block_call(
        mlp_one_finish,
        (shape_of((rows_one, width_one), bfloat), shape_of((rows_two, width_two), bfloat)),
        (
            normed_one,
            other_one,
            bias_one[1],
            partial_one,
            images_par,
            down_bias_one[None],
            scale_one[None],
            gain_mid[None],
            shift_mid[None],
            merge_weight,
            merge_bias[None],
        ),
        [
            pltpu.VMEM((rows_one, width_one), jnp.float32),
            pltpu.VMEM((micro_count * half_rows, 4, half_cols, width_one), bfloat),
        ],
        steps_one,
        ((1, 0), (2, 1)),
    )
    slope_own, slope_other = block_call(
        slope_one_kernel,
        (
            shape_of((rows_one, own_one.shape[0]), bfloat),
            shape_of((rows_one, own_one.shape[0]), bfloat),
        ),
        (normed_one, own_one, other_one, *bias_one),
        [],
        steps_one,
        ((1, 0), (2, 0), (3, 1), (4, 1), ("out0", 1), ("out1", 1)),
    )

    merged_tile = merged.reshape(half_rows, half_cols, width_two)
    normed_two, conv_two = tile_call(
        conv_two_kernel,
        (shape_of((rows_two, width_two), bfloat), shape_of((rows_two, width_two), bfloat)),
        half_rows,
        half_cols,
        width_two,
        (merged_tile, *halo_of(merged_tile, 3), kernel_two, gain_two[None], shift_two[None]),
    )
    grad_rows = grad_out.reshape(rows_two, width_two)
    two_wide = shape_of((rows_two, width_two), jnp.float32)
    two_scratch = pltpu.VMEM((rows_two, width_two), jnp.float32)
    two_branch = pltpu.VMEM((rows_two, width_two), bfloat)
    partial_two, d_partial_two = block_call(
        mlp_two_half,
        (two_wide, two_wide),
        (normed_two, grad_rows, scale_two[None], own_two, bias_two[0]),
        [two_branch],
        steps_two,
        ((3, 0), (4, 1)),
    )
    features, d_conv_two = block_call(
        mlp_two_finish,
        (shape_of((rows_two, width_two), bfloat), shape_of((rows_two, width_two), bfloat)),
        (
            normed_two,
            grad_rows,
            scale_two[None],
            other_two,
            bias_two[1],
            partial_two,
            d_partial_two,
            merged,
            down_bias_two[None],
            conv_two,
            gain_two[None],
        ),
        [two_scratch, two_scratch, two_branch],
        steps_two,
        ((3, 0), (4, 1)),
    )
    back_tile = d_conv_two.reshape(half_rows, half_cols, width_two)
    (d_merged,) = tile_call(
        back_two_kernel,
        (shape_of((rows_two, width_two), bfloat),),
        half_rows,
        half_cols,
        width_two,
        (back_tile, *halo_of(back_tile, 3), kernel_two, grad_rows),
    )
    d_conv_one, upstream_one = block_call(
        back_mlp_one,
        (shape_of((rows_one, width_one), bfloat), shape_of((rows_one, width_one), jnp.float32)),
        (
            d_merged,
            merge_weight,
            section_out,
            gain_mid[None],
            scale_one[None],
            own_one,
            other_one,
            slope_own,
            slope_other,
            conv_one,
            gain_one[None],
        ),
        [
            pltpu.VMEM((rows_one, width_one), bfloat),
            pltpu.VMEM((rows_one, width_one), jnp.float32),
        ],
        steps_one,
        ((5, 0), (6, 0), (7, 1), (8, 1)),
    )
    d_conv_one = d_conv_one.reshape(tile_rows, 2, half_cols, width_one)
    (input_grad,) = tile_call(
        back_one_kernel,
        (shape_of((tile_rows, tile_cols, width_one), bfloat),),
        tile_rows,
        tile_cols,
        width_one,
        (d_conv_one, *halo_of(d_conv_one, 2), kernel_one, upstream_one),
        (pltpu.VMEM((tile_rows, tile_cols, lanes), jnp.float32),),
    )
    return (
        features.reshape(micro_count, half_rows, half_cols, width_two),
        input_grad.reshape(images.shape),
    )


def solution(mesh):
    in_specs = (
        P("sec", "row", "col", None),
        P(),
        P(),
        P(),
        P(None, ("sec", "row", "col")),
        P(),
        P(None, ("sec", "row", "col")),
        P(),
        P(),
        P(),
        P(),
        P(),
        P(),
        P(),
        P(),
        P(),
        P(None, ("sec", "row", "col")),
        P(),
        P(None, ("sec", "row", "col")),
        P(),
        P(),
        P("sec", "row", "col", None),
    )
    out_specs = (P("sec", "row", "col", None), P("sec", "row", "col", None))
    return jax.shard_map(
        on_device, mesh=mesh, in_specs=in_specs, out_specs=out_specs, check_vma=False
    )
```

```python
import jax
import jax.numpy as jnp
from jax import lax
from jax.experimental import pallas as pl
from jax.experimental.pallas import tpu as pltpu
from jax.sharding import PartitionSpec as P

norm_eps = 1e-06


def exchange(block, axis, dim, width):
    count = lax.axis_size(axis)
    forward = [(i, i + 1) for i in range(count - 1)]
    backward = [(target, source) for source, target in forward]
    low = lax.ppermute(
        lax.slice_in_dim(block, block.shape[dim] - width, None, axis=dim), axis, forward
    )
    high = lax.ppermute(lax.slice_in_dim(block, 0, width, axis=dim), axis, backward)
    return low, high


def halo_of(block, width):
    dim = block.ndim - 2
    top, bottom = exchange(block, "row", 0, 3)

    def edge(first, last):
        parts = [lax.slice_in_dim(part, first, last, axis=dim) for part in (top, block, bottom)]
        return jnp.concatenate(parts, axis=0)

    count = lax.axis_size("col")
    extent = block.shape[dim]
    forward = [(i, i + 1) for i in range(count - 1)]
    backward = [(target, source) for source, target in forward]
    left = lax.ppermute(edge(extent - width, extent), "col", forward)
    right = lax.ppermute(edge(0, width), "col", backward)
    return top, bottom, left, right


def ring_collect(piece, axis, inner, stride):
    count = lax.axis_size(axis)
    own_place = (lax.axis_index(axis) // stride) % inner
    found = jnp.zeros((inner, *piece.shape), piece.dtype)
    found = lax.dynamic_update_index_in_dim(found, piece, own_place, 0)
    for shift in range(1, inner):
        pairs = []
        for target in range(count):
            place = (target // stride) % inner
            source = target + ((place + shift) % inner - place) * stride
            pairs.append((source, target))
        arrived = lax.ppermute(piece, axis, pairs)
        found = lax.dynamic_update_index_in_dim(found, arrived, (own_place + shift) % inner, 0)
    return found


def normal_cdf(values):
    return 0.5 * (1.0 + lax.erf(values * 0.7071067811865476))


def slope_from(values, cdf):
    return cdf + values * jnp.exp(-0.5 * values * values) * 0.3989422804014327


def norm_forward(values, norm_gain, norm_shift):
    center = values - jnp.mean(values, axis=-1, keepdims=True)
    inv_std = lax.rsqrt(jnp.mean(center * center, axis=-1, keepdims=True) + norm_eps)
    scaled = center * inv_std
    return (scaled, inv_std, scaled * norm_gain + norm_shift)


def norm_backward(upstream, scaled, inv_std, norm_gain):
    weighted = upstream * norm_gain
    mean_one = jnp.mean(weighted, axis=-1, keepdims=True)
    mean_two = jnp.mean(weighted * scaled, axis=-1, keepdims=True)
    return inv_std * (weighted - mean_one - scaled * mean_two)


def contract_last(left_side, right_side):
    return lax.dot_general(
        left_side, right_side, (((1,), (1,)), ((), ())), preferred_element_type=jnp.float32
    )


lanes = 128


def fill_rows(frame, source, first, width):
    for row in range(source.shape[0]):
        for tile in range(source.shape[-1] // lanes):
            part = source[row, :, tile * lanes : (tile + 1) * lanes].astype(jnp.float32)
            frame[tile, first + row, 8 : 8 + width, :] = part


def fill_edges(frame, left, right, width):
    for row in range(left.shape[0]):
        for tile in range(left.shape[-1] // lanes):
            span = slice(tile * lanes, (tile + 1) * lanes)
            frame[tile, row, 5:8, :] = left[row, :, span].astype(jnp.float32)
            frame[tile, row, 8 + width : 11 + width, :] = right[row, :, span].astype(jnp.float32)


def fill_parity_rows(frame, source, first):
    halves = source.shape[2]
    for row in range(source.shape[0]):
        for tile in range(source.shape[-1] // lanes):
            for parity in range(2):
                part = source[row, parity, :, tile * lanes : (tile + 1) * lanes]
                frame[tile, first + row, pl.ds(8 + parity, halves, stride=2), :] = part.astype(
                    jnp.float32
                )


def fill_parity_edges(frame, left, right, width):
    for row in range(left.shape[0]):
        for tile in range(left.shape[-1] // lanes):
            span = slice(tile * lanes, (tile + 1) * lanes)
            for parity in range(2):
                for half in range(2):
                    col = 2 * half + parity
                    frame[tile, row, 4 + col : 5 + col, :] = left[
                        row, parity, half : half + 1, span
                    ].astype(jnp.float32)
                    frame[tile, row, 8 + width + col : 9 + width + col, :] = right[
                        row, parity, half : half + 1, span
                    ].astype(jnp.float32)


def depthwise(frame, taps, tile, rows, cols, first, stride, flipped):
    sums = [jnp.zeros((cols, lanes), jnp.float32) for _ in range(rows)]
    span = pl.ds(pl.multiple_of(tile * lanes, lanes), lanes)
    for tap_col in range(7):
        weights = [taps[pl.ds(7 * tap_row + tap_col, 1), span] for tap_row in range(7)]
        start = 5 + first + (6 - tap_col if flipped else tap_col)
        for row in range(rows + 6):
            if stride == 1:
                values = frame[tile, row, pl.ds(start, cols), :]
            else:
                values = frame[tile, row, pl.ds(start, cols, stride=stride), :]
            for tap_row in range(7):
                target = row - (6 - tap_row if flipped else tap_row)
                if 0 <= target < rows:
                    sums[target] = sums[target] + values * weights[tap_row]
    return sums


def norm_rows(values_ref, normed_ref, gain_ref, shift_ref, chunk):
    gain = gain_ref[...]
    shift = shift_ref[...]

    def step(index, carry):
        span = pl.ds(pl.multiple_of(index * chunk, chunk), chunk)
        values = values_ref[span, :].astype(jnp.float32)
        normed_ref[span, :] = norm_forward(values, gain, shift)[2].astype(normed_ref.dtype)
        return carry

    lax.fori_loop(0, values_ref.shape[0] // chunk, step, 0)


def conv_one_kernel(
    tile_ref, top, bottom, left, right, taps, gain, shift, normed, conv, residual, frame
):
    rows, width, channels = tile_ref.shape
    halves = width // 2
    fill_rows(frame, top, 0, width)
    fill_rows(frame, tile_ref, 3, width)
    fill_rows(frame, bottom, 3 + rows, width)
    fill_edges(frame, left, right, width)

    def step(tile, carry):
        span = pl.ds(pl.multiple_of(tile * lanes, lanes), lanes)
        for parity in range(2):
            sums = depthwise(frame, taps, tile, rows, halves, parity, 2, False)
            for row in range(rows):
                place = pl.ds(row * width + parity * halves, halves)
                conv[place, span] = sums[row]
                own = frame[tile, 3 + row, pl.ds(8 + parity, halves, stride=2), :]
                residual[place, span] = own.astype(residual.dtype)
        return carry

    lax.fori_loop(0, channels // lanes, step, 0)
    norm_rows(conv, normed, gain, shift, 64)


def back_one_kernel(tile_ref, top, bottom, left, right, taps, upstream, out, frame, total):
    rows, _, halves, channels = tile_ref.shape
    width = 2 * halves
    fill_parity_rows(frame, top, 0)
    fill_parity_rows(frame, tile_ref, 3)
    fill_parity_rows(frame, bottom, 3 + rows)
    fill_parity_edges(frame, left, right, width)

    def step(tile, carry):
        span = pl.ds(pl.multiple_of(tile * lanes, lanes), lanes)
        for parity in range(2):
            sums = depthwise(frame, taps, tile, rows, halves, parity, 2, True)
            for row in range(rows):
                place = pl.ds(row * width + parity * halves, halves)
                total[row, pl.ds(parity, halves, stride=2), :] = sums[row] + upstream[place, span]
        for row in range(rows):
            out[row, :, span] = total[row].astype(out.dtype)
        return carry

    lax.fori_loop(0, channels // lanes, step, 0)


def conv_two_kernel(tile_ref, top, bottom, left, right, taps, gain, shift, normed, conv, frame):
    rows, width, channels = tile_ref.shape
    fill_rows(frame, top, 0, width)
    fill_rows(frame, tile_ref, 3, width)
    fill_rows(frame, bottom, 3 + rows, width)
    fill_edges(frame, left, right, width)

    def step(tile, carry):
        span = pl.ds(pl.multiple_of(tile * lanes, lanes), lanes)
        sums = depthwise(frame, taps, tile, rows, width, 0, 1, False)
        for row in range(rows):
            conv[pl.ds(row * width, width), span] = sums[row].astype(conv.dtype)
        return carry

    lax.fori_loop(0, channels // lanes, step, 0)
    norm_rows(conv, normed, gain, shift, 64)


def back_two_kernel(tile_ref, top, bottom, left, right, taps, grad, out, frame):
    rows, width, channels = tile_ref.shape
    fill_rows(frame, top, 0, width)
    fill_rows(frame, tile_ref, 3, width)
    fill_rows(frame, bottom, 3 + rows, width)
    fill_edges(frame, left, right, width)

    def step(tile, carry):
        span = pl.ds(pl.multiple_of(tile * lanes, lanes), lanes)
        sums = depthwise(frame, taps, tile, rows, width, 0, 1, True)
        for row in range(rows):
            place = pl.ds(row * width, width)
            d_taps = sums[row].astype(jnp.bfloat16).astype(jnp.float32)
            out[place, span] = (d_taps + grad[place, span].astype(jnp.float32)).astype(out.dtype)
        return carry

    lax.fori_loop(0, channels // lanes, step, 0)


def dot(left_side, right_side):
    return jnp.dot(left_side, right_side, preferred_element_type=jnp.float32)


def row_blocks(total, size):
    size = min(total, size)
    return [slice(first, first + size) for first in range(0, total, size)]


def over_hidden(weights, step):
    total = weights.shape[0]
    block = min(total, 256)

    def run(index, carry):
        step(pl.ds(pl.multiple_of(index * block, block), block))
        return carry

    lax.fori_loop(0, total // block, run, 0)


def mlp_one_half(normed, weights, bias, branch):
    width = normed.shape[1]
    branch[...] = jnp.zeros_like(branch)

    def step(units):
        for rows in row_blocks(normed.shape[0], 256):
            pre_act = contract_last(normed[rows, :], weights[units, :width]) + bias[:, units]
            hidden = (pre_act * normal_cdf(pre_act)).astype(jnp.bfloat16)
            branch[rows, :] += dot(hidden, weights[units, width:])

    over_hidden(weights, step)


def mlp_one_finish(
    normed, weights, bias, partial, residual, down_bias, scale, gain, shift, merge, merge_bias,
    section, merged, branch, patches,
):
    mlp_one_half(normed, weights, bias, branch)
    positions, width = normed.shape
    quarter = patches.shape[0]
    half_cols = patches.shape[2]
    step_rows = 4 * half_cols

    def step(index, carry):
        rows = pl.ds(pl.multiple_of(index * step_rows, step_rows), step_rows)
        total = branch[rows, :] + partial[rows, :] + down_bias[...]
        out = (residual[rows, :].astype(jnp.float32) + scale[...] * total).astype(jnp.bfloat16)
        section[rows, :] = out
        normal = norm_forward(out.astype(jnp.float32), gain[...], shift[...])[2]
        normal = normal.astype(jnp.bfloat16)
        for place in range(4):
            patches[index, place] = normal[place * half_cols : (place + 1) * half_cols, :]
        return carry

    lax.fori_loop(0, quarter, step, 0)
    total = merge_bias[...]
    for place in range(4):
        patch = patches[:, place].reshape(quarter * half_cols, width)
        total = total + dot(patch, merge[place * width : (place + 1) * width, :])
    merged[...] = total.astype(merged.dtype)


def slope_one_kernel(normed, own, other, bias_own, bias_other, slope_own, slope_other):
    width = normed.shape[1]

    def step(units):
        for rows in row_blocks(normed.shape[0], 256):
            for weights, bias, slope in (
                (own, bias_own, slope_own),
                (other, bias_other, slope_other),
            ):
                pre_act = contract_last(normed[rows, :], weights[units, :width]) + bias[:, units]
                slope[rows, units] = slope_from(pre_act, normal_cdf(pre_act)).astype(slope.dtype)

    over_hidden(own, step)


def back_mlp_one(
    d_merged, merge, section, gain_mid, scale, own, other, slope_own, slope_other, conv, gain,
    d_conv, upstream, d_branch, d_normed,
):
    width = section.shape[1]
    quarter = d_merged.shape[0]
    groups = section.shape[0] // 64
    half_cols = quarter // groups
    for place in range(4):
        d_normal = contract_last(d_merged[...], merge[place * width : (place + 1) * width, :])
        for group in range(groups):
            first = (4 * group + place) * half_cols
            rows = slice(first, first + half_cols)
            values = section[rows, :].astype(jnp.float32)
            scaled, inv_std, _ = norm_forward(values, 1.0, 0.0)
            flow = norm_backward(
                d_normal[group * half_cols : (group + 1) * half_cols],
                scaled,
                inv_std,
                gain_mid[...],
            )
            upstream[rows, :] = flow
            d_branch[rows, :] = (flow * scale[...]).astype(d_branch.dtype)
    d_normed[...] = jnp.zeros_like(d_normed)

    def step(units):
        for rows in row_blocks(section.shape[0], 256):
            total = d_normed[rows, :]
            for weights, slope in ((own, slope_own), (other, slope_other)):
                d_hidden = contract_last(d_branch[rows, :], weights[units, width:])
                d_pre = (d_hidden * slope[rows, units].astype(jnp.float32)).astype(jnp.bfloat16)
                total = total + dot(d_pre, weights[units, :width])
            d_normed[rows, :] = total

    over_hidden(own, step)
    norm_back_rows(conv, d_normed, gain, d_conv, 64)


def norm_back_rows(conv, d_normed, gain, d_conv, chunk):
    def step(index, carry):
        rows = pl.ds(pl.multiple_of(index * chunk, chunk), chunk)
        scaled, inv_std, _ = norm_forward(conv[rows, :].astype(jnp.float32), 1.0, 0.0)
        flow = norm_backward(d_normed[rows, :], scaled, inv_std, gain[...])
        d_conv[rows, :] = flow.astype(d_conv.dtype)
        return carry

    lax.fori_loop(0, conv.shape[0] // chunk, step, 0)


def mlp_two_half(normed, grad, scale, weights, bias, branch, d_normed, d_branch):
    width = normed.shape[1]
    branch[...] = jnp.zeros_like(branch)
    d_normed[...] = jnp.zeros_like(d_normed)
    d_branch[...] = (grad[...].astype(jnp.float32) * scale[...]).astype(d_branch.dtype)

    def step(units):
        pre_act = contract_last(normed[...], weights[units, :width]) + bias[:, units]
        d_hidden = contract_last(d_branch[...], weights[units, width:])
        cdf = normal_cdf(pre_act)
        hidden = (pre_act * cdf).astype(jnp.bfloat16)
        d_pre = (d_hidden * slope_from(pre_act, cdf)).astype(jnp.bfloat16)
        branch[...] += dot(hidden, weights[units, width:])
        d_normed[...] += dot(d_pre, weights[units, :width])

    over_hidden(weights, step)


def mlp_two_finish(
    normed, grad, scale, weights, bias, partial, d_partial, merged, down_bias, conv, gain,
    features, d_conv, branch, d_normed, d_branch,
):
    mlp_two_half(normed, grad, scale, weights, bias, branch, d_normed, d_branch)
    total = branch[...] + partial[...] + down_bias[...]
    out = merged[...].astype(jnp.float32) + scale[...] * total
    features[...] = out.astype(features.dtype)
    d_normed[...] += d_partial[...]
    norm_back_rows(conv, d_normed, gain, d_conv, 64)


megabyte = 1024 * 1024


def shape_of(dims, dtype):
    return jax.ShapeDtypeStruct(dims, dtype)


def block_call(kernel, outputs, operands, scratch, limit=48):
    whole = pl.BlockSpec(memory_space=pltpu.VMEM)
    return pl.pallas_call(
        kernel,
        out_shape=outputs,
        in_specs=[whole] * len(operands),
        out_specs=[whole] * len(outputs),
        scratch_shapes=scratch,
        compiler_params=pltpu.CompilerParams(vmem_limit_bytes=limit * megabyte),
    )(*operands)


def tile_call(kernel, outputs, rows, width, channels, operands, extra=()):
    frame = pltpu.VMEM((channels // lanes, rows + 6, width + 16, lanes), jnp.float32)
    return block_call(kernel, outputs, operands, [frame, *extra])


def on_device(
    images,
    kernel_one,
    gain_one,
    shift_one,
    up_one,
    up_bias_one,
    down_one,
    down_bias_one,
    scale_one,
    gain_mid,
    shift_mid,
    merge_weight,
    merge_bias,
    kernel_two,
    gain_two,
    shift_two,
    up_two,
    up_bias_two,
    down_two,
    down_bias_two,
    scale_two,
    grad_out,
):
    micro_count, tile_rows, tile_cols, width_one = images.shape
    width_two = merge_weight.shape[1]
    half_rows = tile_rows // 2
    half_cols = tile_cols // 2
    rows_one = micro_count * tile_rows * tile_cols
    rows_two = micro_count * half_rows * half_cols

    swap = [(0, 1), (1, 0)]
    side = lax.axis_index("sec")
    row_count = lax.axis_size("row")
    col_count = lax.axis_size("col")
    inner = 4 if row_count % 4 == 0 else row_count
    outer = row_count // inner
    bfloat = jnp.bfloat16

    def bias_halves(bias):
        halves = bias.reshape(2, 1, -1)
        return (
            jnp.where(side == 0, halves[0], halves[1]),
            jnp.where(side == 0, halves[1], halves[0]),
        )

    share_two = up_two.shape[1]
    packed_one = jnp.concatenate([up_one.T, down_one.T], axis=1)
    packed = jnp.concatenate([up_two.T, down_two.T, packed_one], axis=0)
    column = ring_collect(packed, "col", col_count, 1)
    part_one = column[:, 2 * share_two :].reshape(-1, 2 * width_one)
    part_two = jnp.concatenate(
        [
            column[:, :share_two].reshape(-1, width_two),
            column[:, share_two : 2 * share_two].reshape(-1, width_two),
        ],
        axis=1,
    )
    own_two = lax.all_gather(part_two, "row", axis=0, tiled=True)
    own_one = ring_collect(part_one, "row", inner, 1).reshape(-1, 2 * width_one)
    own_one = ring_collect(own_one, "row", outer, inner).reshape(-1, 2 * width_one)
    bias_one = bias_halves(up_bias_one)
    bias_two = bias_halves(up_bias_two)

    image_tile = images.reshape(tile_rows, tile_cols, width_one)
    normed_one, conv_one, images_par = tile_call(
        conv_one_kernel,
        (
            shape_of((rows_one, width_one), bfloat),
            shape_of((rows_one, width_one), jnp.float32),
            shape_of((rows_one, width_one), bfloat),
        ),
        tile_rows,
        tile_cols,
        width_one,
        (image_tile, *halo_of(image_tile, 3), kernel_one, gain_one[None], shift_one[None]),
    )
    own_one, normed_one, images_par, bias_one, bias_two = lax.optimization_barrier(
        (own_one, normed_one, images_par, bias_one, bias_two)
    )
    other_one = lax.ppermute(own_one, "sec", swap)

    (partial_one,) = block_call(
        mlp_one_half,
        (shape_of((rows_one, width_one), jnp.float32),),
        (normed_one, own_one, bias_one[0]),
        [],
    )
    section_out, merged = block_call(
        mlp_one_finish,
        (shape_of((rows_one, width_one), bfloat), shape_of((rows_two, width_two), bfloat)),
        (
            normed_one,
            other_one,
            bias_one[1],
            partial_one,
            images_par,
            down_bias_one[None],
            scale_one[None],
            gain_mid[None],
            shift_mid[None],
            merge_weight,
            merge_bias[None],
        ),
        [
            pltpu.VMEM((rows_one, width_one), jnp.float32),
            pltpu.VMEM((micro_count * half_rows, 4, half_cols, width_one), bfloat),
        ],
    )
    slope_own, slope_other = block_call(
        slope_one_kernel,
        (
            shape_of((rows_one, own_one.shape[0]), bfloat),
            shape_of((rows_one, own_one.shape[0]), bfloat),
        ),
        (normed_one, own_one, other_one, *bias_one),
        [],
    )

    merged_tile = merged.reshape(half_rows, half_cols, width_two)
    normed_two, conv_two = tile_call(
        conv_two_kernel,
        (shape_of((rows_two, width_two), bfloat), shape_of((rows_two, width_two), bfloat)),
        half_rows,
        half_cols,
        width_two,
        (merged_tile, *halo_of(merged_tile, 3), kernel_two, gain_two[None], shift_two[None]),
    )
    own_two, normed_two = lax.optimization_barrier((own_two, normed_two))
    other_two = lax.ppermute(own_two, "sec", swap)
    grad_rows = grad_out.reshape(rows_two, width_two)
    two_wide = shape_of((rows_two, width_two), jnp.float32)
    two_scratch = pltpu.VMEM((rows_two, width_two), jnp.float32)
    two_branch = pltpu.VMEM((rows_two, width_two), bfloat)
    partial_two, d_partial_two = block_call(
        mlp_two_half,
        (two_wide, two_wide),
        (normed_two, grad_rows, scale_two[None], own_two, bias_two[0]),
        [two_branch],
    )
    features, d_conv_two = block_call(
        mlp_two_finish,
        (shape_of((rows_two, width_two), bfloat), shape_of((rows_two, width_two), bfloat)),
        (
            normed_two,
            grad_rows,
            scale_two[None],
            other_two,
            bias_two[1],
            partial_two,
            d_partial_two,
            merged,
            down_bias_two[None],
            conv_two,
            gain_two[None],
        ),
        [two_scratch, two_scratch, two_branch],
    )
    back_tile = d_conv_two.reshape(half_rows, half_cols, width_two)
    (d_merged,) = tile_call(
        back_two_kernel,
        (shape_of((rows_two, width_two), bfloat),),
        half_rows,
        half_cols,
        width_two,
        (back_tile, *halo_of(back_tile, 3), kernel_two, grad_rows),
    )
    d_conv_one, upstream_one = block_call(
        back_mlp_one,
        (shape_of((rows_one, width_one), bfloat), shape_of((rows_one, width_one), jnp.float32)),
        (
            d_merged,
            merge_weight,
            section_out,
            gain_mid[None],
            scale_one[None],
            own_one,
            other_one,
            slope_own,
            slope_other,
            conv_one,
            gain_one[None],
        ),
        [
            pltpu.VMEM((rows_one, width_one), bfloat),
            pltpu.VMEM((rows_one, width_one), jnp.float32),
        ],
    )
    d_conv_one = d_conv_one.reshape(tile_rows, 2, half_cols, width_one)
    (input_grad,) = tile_call(
        back_one_kernel,
        (shape_of((tile_rows, tile_cols, width_one), bfloat),),
        tile_rows,
        tile_cols,
        width_one,
        (d_conv_one, *halo_of(d_conv_one, 2), kernel_one, upstream_one),
        (pltpu.VMEM((tile_rows, tile_cols, lanes), jnp.float32),),
    )
    return (
        features.reshape(micro_count, half_rows, half_cols, width_two),
        input_grad.reshape(images.shape),
    )


def solution(mesh):
    in_specs = (
        P("sec", "row", "col", None),
        P(),
        P(),
        P(),
        P(None, ("sec", "row", "col")),
        P(),
        P(None, ("sec", "row", "col")),
        P(),
        P(),
        P(),
        P(),
        P(),
        P(),
        P(),
        P(),
        P(),
        P(None, ("sec", "row", "col")),
        P(),
        P(None, ("sec", "row", "col")),
        P(),
        P(),
        P("sec", "row", "col", None),
    )
    out_specs = (P("sec", "row", "col", None), P("sec", "row", "col", None))
    return jax.shard_map(
        on_device, mesh=mesh, in_specs=in_specs, out_specs=out_specs, check_vma=False
    )
```

```python
import jax
import jax.numpy as jnp
from jax import lax
from jax.experimental import pallas as pl
from jax.experimental.pallas import tpu as pltpu
from jax.sharding import PartitionSpec as P

norm_eps = 1e-06


def exchange(block, axis, dim, width):
    count = lax.axis_size(axis)
    forward = [(i, i + 1) for i in range(count - 1)]
    backward = [(target, source) for source, target in forward]
    low = lax.ppermute(
        lax.slice_in_dim(block, block.shape[dim] - width, None, axis=dim), axis, forward
    )
    high = lax.ppermute(lax.slice_in_dim(block, 0, width, axis=dim), axis, backward)
    return low, high


def halo_of(block, width):
    dim = block.ndim - 2
    top, bottom = exchange(block, "row", 0, 3)

    def edge(first, last):
        parts = [lax.slice_in_dim(part, first, last, axis=dim) for part in (top, block, bottom)]
        return jnp.concatenate(parts, axis=0)

    count = lax.axis_size("col")
    extent = block.shape[dim]
    forward = [(i, i + 1) for i in range(count - 1)]
    backward = [(target, source) for source, target in forward]
    left = lax.ppermute(edge(extent - width, extent), "col", forward)
    right = lax.ppermute(edge(0, width), "col", backward)
    return top, bottom, left, right


def ring_collect(piece, axis, inner, stride):
    count = lax.axis_size(axis)
    own_place = (lax.axis_index(axis) // stride) % inner
    found = jnp.zeros((inner, *piece.shape), piece.dtype)
    found = lax.dynamic_update_index_in_dim(found, piece, own_place, 0)
    for shift in range(1, inner):
        pairs = []
        for target in range(count):
            place = (target // stride) % inner
            source = target + ((place + shift) % inner - place) * stride
            pairs.append((source, target))
        arrived = lax.ppermute(piece, axis, pairs)
        found = lax.dynamic_update_index_in_dim(found, arrived, (own_place + shift) % inner, 0)
    return found


def normal_cdf(values):
    return 0.5 * (1.0 + lax.erf(values * 0.7071067811865476))


def slope_from(values, cdf):
    return cdf + values * jnp.exp(-0.5 * values * values) * 0.3989422804014327


def norm_forward(values, norm_gain, norm_shift):
    center = values - jnp.mean(values, axis=-1, keepdims=True)
    inv_std = lax.rsqrt(jnp.mean(center * center, axis=-1, keepdims=True) + norm_eps)
    scaled = center * inv_std
    return (scaled, inv_std, scaled * norm_gain + norm_shift)


def norm_backward(upstream, scaled, inv_std, norm_gain):
    weighted = upstream * norm_gain
    mean_one = jnp.mean(weighted, axis=-1, keepdims=True)
    mean_two = jnp.mean(weighted * scaled, axis=-1, keepdims=True)
    return inv_std * (weighted - mean_one - scaled * mean_two)


def contract_last(left_side, right_side):
    return lax.dot_general(
        left_side, right_side, (((1,), (1,)), ((), ())), preferred_element_type=jnp.float32
    )


lanes = 128


def fill_rows(frame, source, first, width):
    for row in range(source.shape[0]):
        for tile in range(source.shape[-1] // lanes):
            part = source[row, :, tile * lanes : (tile + 1) * lanes].astype(jnp.float32)
            frame[tile, first + row, 8 : 8 + width, :] = part


def fill_edges(frame, left, right, width):
    for row in range(left.shape[0]):
        for tile in range(left.shape[-1] // lanes):
            span = slice(tile * lanes, (tile + 1) * lanes)
            frame[tile, row, 5:8, :] = left[row, :, span].astype(jnp.float32)
            frame[tile, row, 8 + width : 11 + width, :] = right[row, :, span].astype(jnp.float32)


def fill_parity_rows(frame, source, first):
    halves = source.shape[2]
    for row in range(source.shape[0]):
        for tile in range(source.shape[-1] // lanes):
            for parity in range(2):
                part = source[row, parity, :, tile * lanes : (tile + 1) * lanes]
                frame[tile, first + row, pl.ds(8 + parity, halves, stride=2), :] = part.astype(
                    jnp.float32
                )


def fill_parity_edges(frame, left, right, width):
    for row in range(left.shape[0]):
        for tile in range(left.shape[-1] // lanes):
            span = slice(tile * lanes, (tile + 1) * lanes)
            for parity in range(2):
                for half in range(2):
                    col = 2 * half + parity
                    frame[tile, row, 4 + col : 5 + col, :] = left[
                        row, parity, half : half + 1, span
                    ].astype(jnp.float32)
                    frame[tile, row, 8 + width + col : 9 + width + col, :] = right[
                        row, parity, half : half + 1, span
                    ].astype(jnp.float32)


def depthwise(frame, taps, tile, rows, cols, first, stride, flipped):
    sums = [jnp.zeros((cols, lanes), jnp.float32) for _ in range(rows)]
    span = pl.ds(pl.multiple_of(tile * lanes, lanes), lanes)
    for tap_col in range(7):
        weights = [taps[pl.ds(7 * tap_row + tap_col, 1), span] for tap_row in range(7)]
        start = 5 + first + (6 - tap_col if flipped else tap_col)
        for row in range(rows + 6):
            if stride == 1:
                values = frame[tile, row, pl.ds(start, cols), :]
            else:
                values = frame[tile, row, pl.ds(start, cols, stride=stride), :]
            for tap_row in range(7):
                target = row - (6 - tap_row if flipped else tap_row)
                if 0 <= target < rows:
                    sums[target] = sums[target] + values * weights[tap_row]
    return sums


def norm_rows(values_ref, normed_ref, gain_ref, shift_ref, chunk):
    gain = gain_ref[...]
    shift = shift_ref[...]

    def step(index, carry):
        span = pl.ds(pl.multiple_of(index * chunk, chunk), chunk)
        values = values_ref[span, :].astype(jnp.float32)
        normed_ref[span, :] = norm_forward(values, gain, shift)[2].astype(normed_ref.dtype)
        return carry

    lax.fori_loop(0, values_ref.shape[0] // chunk, step, 0)


def conv_one_kernel(
    tile_ref, top, bottom, left, right, taps, gain, shift, normed, conv, residual, frame
):
    rows, width, channels = tile_ref.shape
    halves = width // 2
    fill_rows(frame, top, 0, width)
    fill_rows(frame, tile_ref, 3, width)
    fill_rows(frame, bottom, 3 + rows, width)
    fill_edges(frame, left, right, width)

    def step(tile, carry):
        span = pl.ds(pl.multiple_of(tile * lanes, lanes), lanes)
        for parity in range(2):
            sums = depthwise(frame, taps, tile, rows, halves, parity, 2, False)
            for row in range(rows):
                place = pl.ds(row * width + parity * halves, halves)
                conv[place, span] = sums[row]
                own = frame[tile, 3 + row, pl.ds(8 + parity, halves, stride=2), :]
                residual[place, span] = own.astype(residual.dtype)
        return carry

    lax.fori_loop(0, channels // lanes, step, 0)
    norm_rows(conv, normed, gain, shift, 64)


def back_one_kernel(tile_ref, top, bottom, left, right, taps, upstream, out, frame, total):
    rows, _, halves, channels = tile_ref.shape
    width = 2 * halves
    fill_parity_rows(frame, top, 0)
    fill_parity_rows(frame, tile_ref, 3)
    fill_parity_rows(frame, bottom, 3 + rows)
    fill_parity_edges(frame, left, right, width)

    def step(tile, carry):
        span = pl.ds(pl.multiple_of(tile * lanes, lanes), lanes)
        for parity in range(2):
            sums = depthwise(frame, taps, tile, rows, halves, parity, 2, True)
            for row in range(rows):
                place = pl.ds(row * width + parity * halves, halves)
                total[row, pl.ds(parity, halves, stride=2), :] = sums[row] + upstream[place, span]
        for row in range(rows):
            out[row, :, span] = total[row].astype(out.dtype)
        return carry

    lax.fori_loop(0, channels // lanes, step, 0)


def conv_two_kernel(
    tile_ref, top, bottom, left, right, taps, gain, shift, grad, scale, mine, conv, frame
):
    rows, width, channels = tile_ref.shape
    fill_rows(frame, top, 0, width)
    fill_rows(frame, tile_ref, 3, width)
    fill_rows(frame, bottom, 3 + rows, width)
    fill_edges(frame, left, right, width)

    def step(tile, carry):
        span = pl.ds(pl.multiple_of(tile * lanes, lanes), lanes)
        sums = depthwise(frame, taps, tile, rows, width, 0, 1, False)
        for row in range(rows):
            conv[pl.ds(row * width, width), span] = sums[row].astype(conv.dtype)
        return carry

    lax.fori_loop(0, channels // lanes, step, 0)
    norm_rows(conv, mine, gain, shift, 32)
    count = rows * width
    mine[count:, :] = (grad[...].astype(jnp.float32) * scale[...]).astype(mine.dtype)


def back_two_kernel(tile_ref, top, bottom, left, right, taps, grad, out, frame):
    rows, width, channels = tile_ref.shape
    fill_rows(frame, top, 0, width)
    fill_rows(frame, tile_ref, 3, width)
    fill_rows(frame, bottom, 3 + rows, width)
    fill_edges(frame, left, right, width)

    def step(tile, carry):
        span = pl.ds(pl.multiple_of(tile * lanes, lanes), lanes)
        sums = depthwise(frame, taps, tile, rows, width, 0, 1, True)
        for row in range(rows):
            place = pl.ds(row * width, width)
            d_taps = sums[row].astype(jnp.bfloat16).astype(jnp.float32)
            out[place, span] = (d_taps + grad[place, span].astype(jnp.float32)).astype(out.dtype)
        return carry

    lax.fori_loop(0, channels // lanes, step, 0)


def dot(left_side, right_side):
    return jnp.dot(left_side, right_side, preferred_element_type=jnp.float32)


def row_blocks(total, size):
    size = min(total, size)
    return [slice(first, first + size) for first in range(0, total, size)]


hidden_block = 256


def over_hidden(weights, step, together=1):
    total = weights.shape[0]
    block = min(total, hidden_block)
    together = min(together, total // block)

    def run(index, carry):
        for part in range(together):
            place = index * together + part
            step(place, pl.ds(pl.multiple_of(place * block, block), block))
        return carry

    lax.fori_loop(0, total // block // together, run, 0)


def mlp_one_half(normed, weights, bias, branch):
    width = normed.shape[1]
    branch[...] = jnp.zeros_like(branch)

    def step(place, units):
        for rows in row_blocks(normed.shape[0], 256):
            pre_act = contract_last(normed[rows, :], weights[units, :width]) + bias[:, units]
            hidden = (pre_act * normal_cdf(pre_act)).astype(jnp.bfloat16)
            branch[rows, :] += dot(hidden, weights[units, width:])

    over_hidden(weights, step)


def mlp_one_finish(
    normed, weights, bias, partial, residual, down_bias, scale, gain, shift, merge, merge_bias,
    section, merged, branch, patches,
):
    mlp_one_half(normed, weights, bias, branch)
    positions, width = normed.shape
    quarter = patches.shape[0]
    half_cols = patches.shape[2]
    step_rows = 4 * half_cols

    def step(index, carry):
        rows = pl.ds(pl.multiple_of(index * step_rows, step_rows), step_rows)
        total = branch[rows, :] + partial[rows, :] + down_bias[...]
        out = (residual[rows, :].astype(jnp.float32) + scale[...] * total).astype(jnp.bfloat16)
        section[rows, :] = out
        normal = norm_forward(out.astype(jnp.float32), gain[...], shift[...])[2]
        normal = normal.astype(jnp.bfloat16)
        for place in range(4):
            patches[index, place] = normal[place * half_cols : (place + 1) * half_cols, :]
        return carry

    lax.fori_loop(0, quarter, step, 0)
    total = merge_bias[...]
    for place in range(4):
        patch = patches[:, place].reshape(quarter * half_cols, width)
        total = total + dot(patch, merge[place * width : (place + 1) * width, :])
    merged[...] = total.astype(merged.dtype)


def slope_one_kernel(normed, own, other, bias_own, bias_other, slope_own, slope_other):
    width = normed.shape[1]

    def step(place, units):
        for rows in row_blocks(normed.shape[0], 256):
            for weights, bias, slope in (
                (own, bias_own, slope_own),
                (other, bias_other, slope_other),
            ):
                pre_act = contract_last(normed[rows, :], weights[units, :width]) + bias[:, units]
                slope[place, rows, :] = slope_from(pre_act, normal_cdf(pre_act)).astype(
                    slope.dtype
                )

    over_hidden(own, step)


def back_mlp_one(
    d_merged, merge, section, gain_mid, scale, own, other, slope_own, slope_other, conv, gain,
    d_conv, upstream, d_branch, d_normed,
):
    width = section.shape[1]
    quarter = d_merged.shape[0]
    groups = section.shape[0] // 64
    half_cols = quarter // groups
    for place in range(4):
        d_normal = contract_last(d_merged[...], merge[place * width : (place + 1) * width, :])
        for group in range(groups):
            first = (4 * group + place) * half_cols
            d_normed[first : first + half_cols, :] = d_normal[
                group * half_cols : (group + 1) * half_cols
            ]

    def norm_step(index, carry):
        rows = pl.ds(pl.multiple_of(index * 64, 64), 64)
        scaled, inv_std, _ = norm_forward(section[rows, :].astype(jnp.float32), 1.0, 0.0)
        flow = norm_backward(d_normed[rows, :], scaled, inv_std, gain_mid[...])
        upstream[rows, :] = flow
        d_branch[rows, :] = (flow * scale[...]).astype(d_branch.dtype)
        return carry

    lax.fori_loop(0, groups, norm_step, 0)
    d_normed[...] = jnp.zeros_like(d_normed)

    def step(place, units):
        for rows in row_blocks(section.shape[0], 256):
            total = d_normed[rows, :]
            for weights, slope in ((own, slope_own), (other, slope_other)):
                d_hidden = contract_last(d_branch[rows, :], weights[units, width:])
                d_pre = (d_hidden * slope[place, rows, :].astype(jnp.float32)).astype(jnp.bfloat16)
                total = total + dot(d_pre, weights[units, :width])
            d_normed[rows, :] = total

    over_hidden(own, step)
    norm_back_rows(conv, d_normed, gain, d_conv, 64)


def norm_back_rows(conv, d_normed, gain, d_conv, chunk):
    def step(index, carry):
        rows = pl.ds(pl.multiple_of(index * chunk, chunk), chunk)
        scaled, inv_std, _ = norm_forward(conv[rows, :].astype(jnp.float32), 1.0, 0.0)
        flow = norm_backward(d_normed[rows, :], scaled, inv_std, gain[...])
        d_conv[rows, :] = flow.astype(d_conv.dtype)
        return carry

    lax.fori_loop(0, conv.shape[0] // chunk, step, 0)


def mlp_two_kernel(mine, theirs, weights, bias, keep, send, stacked, d_stacked):
    count = mine.shape[0] // 2
    width = mine.shape[1]
    for first, source in ((0, mine), (count, theirs)):
        stacked[first : first + count, :] = source[:count, :]
        d_stacked[first : first + count, :] = source[count:, :]
    keep[...] = jnp.zeros_like(keep)
    send[...] = jnp.zeros_like(send)

    def step(place, units):
        pre_act = contract_last(stacked[...], weights[units, :width]) + bias[:, units]
        d_hidden = contract_last(d_stacked[...], weights[units, width:])
        cdf = normal_cdf(pre_act)
        hidden = (pre_act * cdf).astype(jnp.bfloat16)
        d_pre = (d_hidden * slope_from(pre_act, cdf)).astype(jnp.bfloat16)
        branch = dot(hidden, weights[units, width:])
        d_normed = dot(d_pre, weights[units, :width])
        keep[:count, :] += branch[:count]
        send[:count, :] += branch[count:]
        keep[count:, :] += d_normed[:count]
        send[count:, :] += d_normed[count:]

    over_hidden(weights, step, 2)


def two_finish_kernel(keep, back, merged, scale, down_bias, conv, gain, features, d_conv):
    count = merged.shape[0]

    def step(index, carry):
        rows = pl.ds(pl.multiple_of(index * 32, 32), 32)
        low = pl.ds(pl.multiple_of(count + index * 32, 32), 32)
        total = keep[rows, :] + back[rows, :] + down_bias[...]
        out = merged[rows, :].astype(jnp.float32) + scale[...] * total
        features[rows, :] = out.astype(features.dtype)
        scaled, inv_std, _ = norm_forward(conv[rows, :].astype(jnp.float32), 1.0, 0.0)
        flow = norm_backward(keep[low, :] + back[low, :], scaled, inv_std, gain[...])
        d_conv[rows, :] = flow.astype(d_conv.dtype)
        return carry

    lax.fori_loop(0, count // 32, step, 0)


megabyte = 1024 * 1024


def shape_of(dims, dtype):
    return jax.ShapeDtypeStruct(dims, dtype)


def block_call(kernel, outputs, operands, scratch, limit=48):
    whole = pl.BlockSpec(memory_space=pltpu.VMEM)
    return pl.pallas_call(
        kernel,
        out_shape=outputs,
        in_specs=[whole] * len(operands),
        out_specs=[whole] * len(outputs),
        scratch_shapes=scratch,
        compiler_params=pltpu.CompilerParams(vmem_limit_bytes=limit * megabyte),
    )(*operands)


def tile_call(kernel, outputs, rows, width, channels, operands, extra=()):
    frame = pltpu.VMEM((channels // lanes, rows + 6, width + 16, lanes), jnp.float32)
    return block_call(kernel, outputs, operands, [frame, *extra])


def on_device(
    images,
    kernel_one,
    gain_one,
    shift_one,
    up_one,
    up_bias_one,
    down_one,
    down_bias_one,
    scale_one,
    gain_mid,
    shift_mid,
    merge_weight,
    merge_bias,
    kernel_two,
    gain_two,
    shift_two,
    up_two,
    up_bias_two,
    down_two,
    down_bias_two,
    scale_two,
    grad_out,
):
    micro_count, tile_rows, tile_cols, width_one = images.shape
    width_two = merge_weight.shape[1]
    half_rows = tile_rows // 2
    half_cols = tile_cols // 2
    rows_one = micro_count * tile_rows * tile_cols
    rows_two = micro_count * half_rows * half_cols

    swap = [(0, 1), (1, 0)]
    side = lax.axis_index("sec")
    row_count = lax.axis_size("row")
    col_count = lax.axis_size("col")
    inner = 4 if row_count % 4 == 0 else row_count
    outer = row_count // inner
    bfloat = jnp.bfloat16

    def bias_halves(bias):
        halves = bias.reshape(2, 1, -1)
        return (
            jnp.where(side == 0, halves[0], halves[1]),
            jnp.where(side == 0, halves[1], halves[0]),
        )

    share_two = up_two.shape[1]
    packed_one = jnp.concatenate([up_one.T, down_one.T], axis=1)
    packed = jnp.concatenate([up_two.T, down_two.T, packed_one], axis=0)
    column = ring_collect(packed, "col", col_count, 1)
    part_one = column[:, 2 * share_two :].reshape(-1, 2 * width_one)
    part_two = jnp.concatenate(
        [
            column[:, :share_two].reshape(-1, width_two),
            column[:, share_two : 2 * share_two].reshape(-1, width_two),
        ],
        axis=1,
    )
    own_two = lax.all_gather(part_two, "row", axis=0, tiled=True)
    own_one = ring_collect(part_one, "row", inner, 1).reshape(-1, 2 * width_one)
    own_one = ring_collect(own_one, "row", outer, inner).reshape(-1, 2 * width_one)
    bias_one = bias_halves(up_bias_one)
    bias_two = bias_halves(up_bias_two)

    image_tile = images.reshape(tile_rows, tile_cols, width_one)
    normed_one, conv_one, images_par = tile_call(
        conv_one_kernel,
        (
            shape_of((rows_one, width_one), bfloat),
            shape_of((rows_one, width_one), jnp.float32),
            shape_of((rows_one, width_one), bfloat),
        ),
        tile_rows,
        tile_cols,
        width_one,
        (image_tile, *halo_of(image_tile, 3), kernel_one, gain_one[None], shift_one[None]),
    )
    flat = tuple(
        vector[None]
        for vector in (
            down_bias_one, scale_one, gain_mid, shift_mid, merge_bias, gain_two, shift_two,
            scale_two, down_bias_two, gain_one,
        )
    )
    own_one, normed_one, images_par, bias_one, bias_two, flat = lax.optimization_barrier(
        (own_one, normed_one, images_par, bias_one, bias_two, flat)
    )
    (
        flat_down_one, flat_scale_one, flat_gain_mid, flat_shift_mid, flat_merge_bias,
        flat_gain_two, flat_shift_two, flat_scale_two, flat_down_two, flat_gain_one,
    ) = flat
    other_one = lax.ppermute(own_one, "sec", swap)

    (partial_one,) = block_call(
        mlp_one_half,
        (shape_of((rows_one, width_one), jnp.float32),),
        (normed_one, own_one, bias_one[0]),
        [],
    )
    section_out, merged = block_call(
        mlp_one_finish,
        (shape_of((rows_one, width_one), bfloat), shape_of((rows_two, width_two), bfloat)),
        (
            normed_one,
            other_one,
            bias_one[1],
            partial_one,
            images_par,
            flat_down_one,
            flat_scale_one,
            flat_gain_mid,
            flat_shift_mid,
            merge_weight,
            flat_merge_bias,
        ),
        [
            pltpu.VMEM((rows_one, width_one), jnp.float32),
            pltpu.VMEM((micro_count * half_rows, 4, half_cols, width_one), bfloat),
        ],
    )
    block = min(own_one.shape[0], hidden_block)
    slope_dims = (own_one.shape[0] // block, rows_one, block)
    slope_own, slope_other = block_call(
        slope_one_kernel,
        (shape_of(slope_dims, bfloat), shape_of(slope_dims, bfloat)),
        (normed_one, own_one, other_one, *bias_one),
        [],
    )

    merged_tile = merged.reshape(half_rows, half_cols, width_two)
    grad_rows = grad_out.reshape(rows_two, width_two)
    mine, conv_two = tile_call(
        conv_two_kernel,
        (shape_of((2 * rows_two, width_two), bfloat), shape_of((rows_two, width_two), bfloat)),
        half_rows,
        half_cols,
        width_two,
        (
            merged_tile,
            *halo_of(merged_tile, 3),
            kernel_two,
            flat_gain_two,
            flat_shift_two,
            grad_rows,
            flat_scale_two,
        ),
    )
    mine, own_two = lax.optimization_barrier((mine, own_two))
    theirs = lax.ppermute(mine, "sec", swap)
    both_dims = (2 * rows_two, width_two)
    keep, send = block_call(
        mlp_two_kernel,
        (shape_of(both_dims, jnp.float32), shape_of(both_dims, jnp.float32)),
        (mine, theirs, own_two, bias_two[0]),
        [pltpu.VMEM(both_dims, bfloat), pltpu.VMEM(both_dims, bfloat)],
    )
    back = lax.ppermute(send, "sec", swap)
    features, d_conv_two = block_call(
        two_finish_kernel,
        (shape_of((rows_two, width_two), bfloat), shape_of((rows_two, width_two), bfloat)),
        (keep, back, merged, flat_scale_two, flat_down_two, conv_two, flat_gain_two),
        [],
    )
    back_tile = d_conv_two.reshape(half_rows, half_cols, width_two)
    (d_merged,) = tile_call(
        back_two_kernel,
        (shape_of((rows_two, width_two), bfloat),),
        half_rows,
        half_cols,
        width_two,
        (back_tile, *halo_of(back_tile, 3), kernel_two, grad_rows),
    )
    d_conv_one, upstream_one = block_call(
        back_mlp_one,
        (shape_of((rows_one, width_one), bfloat), shape_of((rows_one, width_one), jnp.float32)),
        (
            d_merged,
            merge_weight,
            section_out,
            flat_gain_mid,
            flat_scale_one,
            own_one,
            other_one,
            slope_own,
            slope_other,
            conv_one,
            flat_gain_one,
        ),
        [
            pltpu.VMEM((rows_one, width_one), bfloat),
            pltpu.VMEM((rows_one, width_one), jnp.float32),
        ],
    )
    d_conv_one = d_conv_one.reshape(tile_rows, 2, half_cols, width_one)
    (input_grad,) = tile_call(
        back_one_kernel,
        (shape_of((tile_rows, tile_cols, width_one), bfloat),),
        tile_rows,
        tile_cols,
        width_one,
        (d_conv_one, *halo_of(d_conv_one, 2), kernel_one, upstream_one),
        (pltpu.VMEM((tile_rows, tile_cols, lanes), jnp.float32),),
    )
    return (
        features.reshape(micro_count, half_rows, half_cols, width_two),
        input_grad.reshape(images.shape),
    )


def solution(mesh):
    in_specs = (
        P("sec", "row", "col", None),
        P(),
        P(),
        P(),
        P(None, ("sec", "row", "col")),
        P(),
        P(None, ("sec", "row", "col")),
        P(),
        P(),
        P(),
        P(),
        P(),
        P(),
        P(),
        P(),
        P(),
        P(None, ("sec", "row", "col")),
        P(),
        P(None, ("sec", "row", "col")),
        P(),
        P(),
        P("sec", "row", "col", None),
    )
    out_specs = (P("sec", "row", "col", None), P("sec", "row", "col", None))
    return jax.shard_map(
        on_device, mesh=mesh, in_specs=in_specs, out_specs=out_specs, check_vma=False
    )
```

```python
import jax
import jax.numpy as jnp
from jax import lax
from jax.experimental import pallas as pl
from jax.experimental.pallas import tpu as pltpu
from jax.sharding import PartitionSpec as P

norm_eps = 1e-06


def exchange(block, axis, dim, width):
    count = lax.axis_size(axis)
    forward = [(i, i + 1) for i in range(count - 1)]
    backward = [(target, source) for source, target in forward]
    low = lax.ppermute(
        lax.slice_in_dim(block, block.shape[dim] - width, None, axis=dim), axis, forward
    )
    high = lax.ppermute(lax.slice_in_dim(block, 0, width, axis=dim), axis, backward)
    return low, high


def halo_of(block, width):
    dim = block.ndim - 2
    top, bottom = exchange(block, "row", 0, 3)

    def edge(first, last):
        parts = [lax.slice_in_dim(part, first, last, axis=dim) for part in (top, block, bottom)]
        return jnp.concatenate(parts, axis=0)

    count = lax.axis_size("col")
    extent = block.shape[dim]
    forward = [(i, i + 1) for i in range(count - 1)]
    backward = [(target, source) for source, target in forward]
    left = lax.ppermute(edge(extent - width, extent), "col", forward)
    right = lax.ppermute(edge(0, width), "col", backward)
    return top, bottom, left, right


def ring_collect(piece, axis, inner, stride):
    count = lax.axis_size(axis)
    own_place = (lax.axis_index(axis) // stride) % inner
    found = jnp.zeros((inner, *piece.shape), piece.dtype)
    found = lax.dynamic_update_index_in_dim(found, piece, own_place, 0)
    for shift in range(1, inner):
        pairs = []
        for target in range(count):
            place = (target // stride) % inner
            source = target + ((place + shift) % inner - place) * stride
            pairs.append((source, target))
        arrived = lax.ppermute(piece, axis, pairs)
        found = lax.dynamic_update_index_in_dim(found, arrived, (own_place + shift) % inner, 0)
    return found


def normal_cdf(values):
    return 0.5 * (1.0 + lax.erf(values * 0.7071067811865476))


def slope_from(values, cdf):
    return cdf + values * jnp.exp(-0.5 * values * values) * 0.3989422804014327


def norm_forward(values, norm_gain, norm_shift):
    center = values - jnp.mean(values, axis=-1, keepdims=True)
    inv_std = lax.rsqrt(jnp.mean(center * center, axis=-1, keepdims=True) + norm_eps)
    scaled = center * inv_std
    return (scaled, inv_std, scaled * norm_gain + norm_shift)


def norm_backward(upstream, scaled, inv_std, norm_gain):
    weighted = upstream * norm_gain
    mean_one = jnp.mean(weighted, axis=-1, keepdims=True)
    mean_two = jnp.mean(weighted * scaled, axis=-1, keepdims=True)
    return inv_std * (weighted - mean_one - scaled * mean_two)


def contract_last(left_side, right_side):
    return lax.dot_general(
        left_side, right_side, (((1,), (1,)), ((), ())), preferred_element_type=jnp.float32
    )


lanes = 128


def fill_rows(frame, source, first, width):
    for row in range(source.shape[0]):
        for tile in range(source.shape[-1] // lanes):
            part = source[row, :, tile * lanes : (tile + 1) * lanes].astype(jnp.float32)
            frame[tile, first + row, 8 : 8 + width, :] = part


def fill_edges(frame, left, right, width):
    for row in range(left.shape[0]):
        for tile in range(left.shape[-1] // lanes):
            span = slice(tile * lanes, (tile + 1) * lanes)
            frame[tile, row, 5:8, :] = left[row, :, span].astype(jnp.float32)
            frame[tile, row, 8 + width : 11 + width, :] = right[row, :, span].astype(jnp.float32)


def fill_parity_rows(frame, source, first):
    halves = source.shape[2]
    for row in range(source.shape[0]):
        for tile in range(source.shape[-1] // lanes):
            for parity in range(2):
                part = source[row, parity, :, tile * lanes : (tile + 1) * lanes]
                frame[tile, first + row, pl.ds(8 + parity, halves, stride=2), :] = part.astype(
                    jnp.float32
                )


def fill_parity_edges(frame, left, right, width):
    for row in range(left.shape[0]):
        for tile in range(left.shape[-1] // lanes):
            span = slice(tile * lanes, (tile + 1) * lanes)
            for parity in range(2):
                for half in range(2):
                    col = 2 * half + parity
                    frame[tile, row, 4 + col : 5 + col, :] = left[
                        row, parity, half : half + 1, span
                    ].astype(jnp.float32)
                    frame[tile, row, 8 + width + col : 9 + width + col, :] = right[
                        row, parity, half : half + 1, span
                    ].astype(jnp.float32)


def depthwise(frame, taps, tile, rows, cols, first, stride, flipped):
    sums = [jnp.zeros((cols, lanes), jnp.float32) for _ in range(rows)]
    span = pl.ds(pl.multiple_of(tile * lanes, lanes), lanes)
    for tap_col in range(7):
        weights = [taps[pl.ds(7 * tap_row + tap_col, 1), span] for tap_row in range(7)]
        start = 5 + first + (6 - tap_col if flipped else tap_col)
        for row in range(rows + 6):
            if stride == 1:
                values = frame[tile, row, pl.ds(start, cols), :]
            else:
                values = frame[tile, row, pl.ds(start, cols, stride=stride), :]
            for tap_row in range(7):
                target = row - (6 - tap_row if flipped else tap_row)
                if 0 <= target < rows:
                    sums[target] = sums[target] + values * weights[tap_row]
    return sums


def norm_rows(values_ref, normed_ref, gain_ref, shift_ref, chunk):
    gain = gain_ref[...]
    shift = shift_ref[...]

    for first in range(0, values_ref.shape[0], chunk):
        span = slice(first, first + chunk)
        values = values_ref[span, :].astype(jnp.float32)
        normed_ref[span, :] = norm_forward(values, gain, shift)[2].astype(normed_ref.dtype)


def conv_one_kernel(
    tile_ref, top, bottom, left, right, taps, gain, shift, normed, conv, residual, frame
):
    rows, width, channels = tile_ref.shape
    halves = width // 2
    fill_rows(frame, top, 0, width)
    fill_rows(frame, tile_ref, 3, width)
    fill_rows(frame, bottom, 3 + rows, width)
    fill_edges(frame, left, right, width)

    def step(tile, carry):
        span = pl.ds(pl.multiple_of(tile * lanes, lanes), lanes)
        for parity in range(2):
            sums = depthwise(frame, taps, tile, rows, halves, parity, 2, False)
            for row in range(rows):
                place = pl.ds(row * width + parity * halves, halves)
                conv[place, span] = sums[row]
                own = frame[tile, 3 + row, pl.ds(8 + parity, halves, stride=2), :]
                residual[place, span] = own.astype(residual.dtype)
        return carry

    lax.fori_loop(0, channels // lanes, step, 0)
    norm_rows(conv, normed, gain, shift, 32)


def back_one_kernel(tile_ref, top, bottom, left, right, taps, upstream, out, frame, total):
    rows, _, halves, channels = tile_ref.shape
    width = 2 * halves
    fill_parity_rows(frame, top, 0)
    fill_parity_rows(frame, tile_ref, 3)
    fill_parity_rows(frame, bottom, 3 + rows)
    fill_parity_edges(frame, left, right, width)

    def step(tile, carry):
        span = pl.ds(pl.multiple_of(tile * lanes, lanes), lanes)
        for parity in range(2):
            sums = depthwise(frame, taps, tile, rows, halves, parity, 2, True)
            for row in range(rows):
                place = pl.ds(row * width + parity * halves, halves)
                total[row, pl.ds(parity, halves, stride=2), :] = sums[row] + upstream[place, span]
        for row in range(rows):
            out[row, :, span] = total[row].astype(out.dtype)
        return carry

    lax.fori_loop(0, channels // lanes, step, 0)


def conv_two_kernel(
    tile_ref, top, bottom, left, right, taps, gain, shift, grad, scale, mine, conv, frame
):
    rows, width, channels = tile_ref.shape
    fill_rows(frame, top, 0, width)
    fill_rows(frame, tile_ref, 3, width)
    fill_rows(frame, bottom, 3 + rows, width)
    fill_edges(frame, left, right, width)

    def step(tile, carry):
        span = pl.ds(pl.multiple_of(tile * lanes, lanes), lanes)
        sums = depthwise(frame, taps, tile, rows, width, 0, 1, False)
        for row in range(rows):
            conv[pl.ds(row * width, width), span] = sums[row].astype(conv.dtype)
        return carry

    lax.fori_loop(0, channels // lanes, step, 0)
    norm_rows(conv, mine, gain, shift, 32)
    count = rows * width
    mine[count:, :] = (grad[...].astype(jnp.float32) * scale[...]).astype(mine.dtype)


def back_two_kernel(tile_ref, top, bottom, left, right, taps, grad, out, frame):
    rows, width, channels = tile_ref.shape
    fill_rows(frame, top, 0, width)
    fill_rows(frame, tile_ref, 3, width)
    fill_rows(frame, bottom, 3 + rows, width)
    fill_edges(frame, left, right, width)

    def step(tile, carry):
        span = pl.ds(pl.multiple_of(tile * lanes, lanes), lanes)
        sums = depthwise(frame, taps, tile, rows, width, 0, 1, True)
        for row in range(rows):
            place = pl.ds(row * width, width)
            d_taps = sums[row].astype(jnp.bfloat16).astype(jnp.float32)
            out[place, span] = (d_taps + grad[place, span].astype(jnp.float32)).astype(out.dtype)
        return carry

    lax.fori_loop(0, channels // lanes, step, 0)


def dot(left_side, right_side):
    return jnp.dot(left_side, right_side, preferred_element_type=jnp.float32)


def row_blocks(total, size):
    size = min(total, size)
    return [slice(first, first + size) for first in range(0, total, size)]


hidden_block = 256


def over_hidden(weights, step, together=1):
    total = weights.shape[0]
    block = min(total, hidden_block)
    together = min(together, total // block)

    def run(index, carry):
        for part in range(together):
            place = index * together + part
            step(place, pl.ds(pl.multiple_of(place * block, block), block))
        return carry

    lax.fori_loop(0, total // block // together, run, 0)


def mlp_one_half(normed, weights, bias, branch):
    width = normed.shape[1]
    branch[...] = jnp.zeros_like(branch)

    def step(place, units):
        for rows in row_blocks(normed.shape[0], 256):
            pre_act = contract_last(normed[rows, :], weights[units, :width]) + bias[:, units]
            hidden = (pre_act * normal_cdf(pre_act)).astype(jnp.bfloat16)
            branch[rows, :] += dot(hidden, weights[units, width:])

    over_hidden(weights, step)


def mlp_one_finish(
    normed, weights, bias, partial, residual, down_bias, scale, gain, shift, merge, merge_bias,
    section, merged, branch, patches,
):
    mlp_one_half(normed, weights, bias, branch)
    positions, width = normed.shape
    quarter = patches.shape[0]
    half_cols = patches.shape[2]
    step_rows = 4 * half_cols

    for index in range(quarter):
        rows = slice(index * step_rows, (index + 1) * step_rows)
        total = branch[rows, :] + partial[rows, :] + down_bias[...]
        out = (residual[rows, :].astype(jnp.float32) + scale[...] * total).astype(jnp.bfloat16)
        section[rows, :] = out
        normal = norm_forward(out.astype(jnp.float32), gain[...], shift[...])[2]
        normal = normal.astype(jnp.bfloat16)
        for place in range(4):
            patches[index, place] = normal[place * half_cols : (place + 1) * half_cols, :]

    total = merge_bias[...]
    for place in range(4):
        patch = patches[:, place].reshape(quarter * half_cols, width)
        total = total + dot(patch, merge[place * width : (place + 1) * width, :])
    merged[...] = total.astype(merged.dtype)


def slope_one_kernel(normed, own, other, bias_own, bias_other, slope_own, slope_other):
    width = normed.shape[1]

    def step(place, units):
        for rows in row_blocks(normed.shape[0], 256):
            for weights, bias, slope in (
                (own, bias_own, slope_own),
                (other, bias_other, slope_other),
            ):
                pre_act = contract_last(normed[rows, :], weights[units, :width]) + bias[:, units]
                slope[place, rows, :] = slope_from(pre_act, normal_cdf(pre_act)).astype(
                    slope.dtype
                )

    over_hidden(own, step)


def back_mlp_one(
    d_merged, merge, section, gain_mid, scale, own, other, slope_own, slope_other, conv, gain,
    d_conv, upstream, d_branch, d_normed,
):
    width = section.shape[1]
    quarter = d_merged.shape[0]
    groups = section.shape[0] // 64
    half_cols = quarter // groups
    for place in range(4):
        d_normal = contract_last(d_merged[...], merge[place * width : (place + 1) * width, :])
        for group in range(groups):
            first = (4 * group + place) * half_cols
            rows = slice(first, first + half_cols)
            scaled, inv_std, _ = norm_forward(section[rows, :].astype(jnp.float32), 1.0, 0.0)
            flow = norm_backward(
                d_normal[group * half_cols : (group + 1) * half_cols],
                scaled,
                inv_std,
                gain_mid[...],
            )
            upstream[rows, :] = flow
            d_branch[rows, :] = (flow * scale[...]).astype(d_branch.dtype)
    d_normed[...] = jnp.zeros_like(d_normed)

    def step(place, units):
        for rows in row_blocks(section.shape[0], 256):
            total = d_normed[rows, :]
            for weights, slope in ((own, slope_own), (other, slope_other)):
                d_hidden = contract_last(d_branch[rows, :], weights[units, width:])
                d_pre = (d_hidden * slope[place, rows, :].astype(jnp.float32)).astype(jnp.bfloat16)
                total = total + dot(d_pre, weights[units, :width])
            d_normed[rows, :] = total

    over_hidden(own, step)
    norm_back_rows(conv, d_normed, gain, d_conv, 32)


def norm_back_rows(conv, d_normed, gain, d_conv, chunk):
    for first in range(0, conv.shape[0], chunk):
        rows = slice(first, first + chunk)
        scaled, inv_std, _ = norm_forward(conv[rows, :].astype(jnp.float32), 1.0, 0.0)
        flow = norm_backward(d_normed[rows, :], scaled, inv_std, gain[...])
        d_conv[rows, :] = flow.astype(d_conv.dtype)


def mlp_two_kernel(mine, theirs, weights, bias, keep, send, stacked, d_stacked):
    count = mine.shape[0] // 2
    width = mine.shape[1]
    for first, source in ((0, mine), (count, theirs)):
        stacked[first : first + count, :] = source[:count, :]
        d_stacked[first : first + count, :] = source[count:, :]
    keep[...] = jnp.zeros_like(keep)
    send[...] = jnp.zeros_like(send)

    def step(place, units):
        pre_act = contract_last(stacked[...], weights[units, :width]) + bias[:, units]
        d_hidden = contract_last(d_stacked[...], weights[units, width:])
        cdf = normal_cdf(pre_act)
        hidden = (pre_act * cdf).astype(jnp.bfloat16)
        d_pre = (d_hidden * slope_from(pre_act, cdf)).astype(jnp.bfloat16)
        branch = dot(hidden, weights[units, width:])
        d_normed = dot(d_pre, weights[units, :width])
        keep[:count, :] += branch[:count]
        send[:count, :] += branch[count:]
        keep[count:, :] += d_normed[:count]
        send[count:, :] += d_normed[count:]

    over_hidden(weights, step, 2)


def two_finish_kernel(keep, back, merged, scale, down_bias, conv, gain, features, d_conv):
    count = merged.shape[0]

    for first in range(0, count, 32):
        rows = slice(first, first + 32)
        low = slice(count + first, count + first + 32)
        total = keep[rows, :] + back[rows, :] + down_bias[...]
        out = merged[rows, :].astype(jnp.float32) + scale[...] * total
        features[rows, :] = out.astype(features.dtype)
        scaled, inv_std, _ = norm_forward(conv[rows, :].astype(jnp.float32), 1.0, 0.0)
        flow = norm_backward(keep[low, :] + back[low, :], scaled, inv_std, gain[...])
        d_conv[rows, :] = flow.astype(d_conv.dtype)


megabyte = 1024 * 1024


def shape_of(dims, dtype):
    return jax.ShapeDtypeStruct(dims, dtype)


def block_call(kernel, outputs, operands, scratch, limit=48):
    whole = pl.BlockSpec(memory_space=pltpu.VMEM)
    return pl.pallas_call(
        kernel,
        out_shape=outputs,
        in_specs=[whole] * len(operands),
        out_specs=[whole] * len(outputs),
        scratch_shapes=scratch,
        compiler_params=pltpu.CompilerParams(vmem_limit_bytes=limit * megabyte),
    )(*operands)


def tile_call(kernel, outputs, rows, width, channels, operands, extra=()):
    frame = pltpu.VMEM((channels // lanes, rows + 6, width + 16, lanes), jnp.float32)
    return block_call(kernel, outputs, operands, [frame, *extra])


def on_device(
    images,
    kernel_one,
    gain_one,
    shift_one,
    up_one,
    up_bias_one,
    down_one,
    down_bias_one,
    scale_one,
    gain_mid,
    shift_mid,
    merge_weight,
    merge_bias,
    kernel_two,
    gain_two,
    shift_two,
    up_two,
    up_bias_two,
    down_two,
    down_bias_two,
    scale_two,
    grad_out,
):
    micro_count, tile_rows, tile_cols, width_one = images.shape
    width_two = merge_weight.shape[1]
    half_rows = tile_rows // 2
    half_cols = tile_cols // 2
    rows_one = micro_count * tile_rows * tile_cols
    rows_two = micro_count * half_rows * half_cols

    swap = [(0, 1), (1, 0)]
    side = lax.axis_index("sec")
    row_count = lax.axis_size("row")
    col_count = lax.axis_size("col")
    inner = 4 if row_count % 4 == 0 else row_count
    outer = row_count // inner
    bfloat = jnp.bfloat16

    def bias_halves(bias):
        halves = bias.reshape(2, 1, -1)
        return (
            jnp.where(side == 0, halves[0], halves[1]),
            jnp.where(side == 0, halves[1], halves[0]),
        )

    share_two = up_two.shape[1]
    packed_one = jnp.concatenate([up_one.T, down_one.T], axis=1)
    packed = jnp.concatenate([up_two.T, down_two.T, packed_one], axis=0)
    column = ring_collect(packed, "col", col_count, 1)
    part_one = column[:, 2 * share_two :].reshape(-1, 2 * width_one)
    part_two = jnp.concatenate(
        [
            column[:, :share_two].reshape(-1, width_two),
            column[:, share_two : 2 * share_two].reshape(-1, width_two),
        ],
        axis=1,
    )
    own_two = lax.all_gather(part_two, "row", axis=0, tiled=True)
    own_one = ring_collect(part_one, "row", inner, 1).reshape(-1, 2 * width_one)
    own_one = ring_collect(own_one, "row", outer, inner).reshape(-1, 2 * width_one)
    bias_one = bias_halves(up_bias_one)
    bias_two = bias_halves(up_bias_two)

    image_tile = images.reshape(tile_rows, tile_cols, width_one)
    normed_one, conv_one, images_par = tile_call(
        conv_one_kernel,
        (
            shape_of((rows_one, width_one), bfloat),
            shape_of((rows_one, width_one), jnp.float32),
            shape_of((rows_one, width_one), bfloat),
        ),
        tile_rows,
        tile_cols,
        width_one,
        (image_tile, *halo_of(image_tile, 3), kernel_one, gain_one[None], shift_one[None]),
    )
    flat = tuple(
        vector[None]
        for vector in (
            down_bias_one, scale_one, gain_mid, shift_mid, merge_bias, gain_two, shift_two,
            scale_two, down_bias_two, gain_one,
        )
    )
    own_one, normed_one, images_par, bias_one, bias_two, flat = lax.optimization_barrier(
        (own_one, normed_one, images_par, bias_one, bias_two, flat)
    )
    (
        flat_down_one, flat_scale_one, flat_gain_mid, flat_shift_mid, flat_merge_bias,
        flat_gain_two, flat_shift_two, flat_scale_two, flat_down_two, flat_gain_one,
    ) = flat
    other_one = lax.ppermute(own_one, "sec", swap)

    (partial_one,) = block_call(
        mlp_one_half,
        (shape_of((rows_one, width_one), jnp.float32),),
        (normed_one, own_one, bias_one[0]),
        [],
    )
    section_out, merged = block_call(
        mlp_one_finish,
        (shape_of((rows_one, width_one), bfloat), shape_of((rows_two, width_two), bfloat)),
        (
            normed_one,
            other_one,
            bias_one[1],
            partial_one,
            images_par,
            flat_down_one,
            flat_scale_one,
            flat_gain_mid,
            flat_shift_mid,
            merge_weight,
            flat_merge_bias,
        ),
        [
            pltpu.VMEM((rows_one, width_one), jnp.float32),
            pltpu.VMEM((micro_count * half_rows, 4, half_cols, width_one), bfloat),
        ],
    )
    block = min(own_one.shape[0], hidden_block)
    slope_dims = (own_one.shape[0] // block, rows_one, block)
    slope_own, slope_other = block_call(
        slope_one_kernel,
        (shape_of(slope_dims, bfloat), shape_of(slope_dims, bfloat)),
        (normed_one, own_one, other_one, *bias_one),
        [],
    )

    merged_tile = merged.reshape(half_rows, half_cols, width_two)
    grad_rows = grad_out.reshape(rows_two, width_two)
    mine, conv_two = tile_call(
        conv_two_kernel,
        (shape_of((2 * rows_two, width_two), bfloat), shape_of((rows_two, width_two), bfloat)),
        half_rows,
        half_cols,
        width_two,
        (
            merged_tile,
            *halo_of(merged_tile, 3),
            kernel_two,
            flat_gain_two,
            flat_shift_two,
            grad_rows,
            flat_scale_two,
        ),
    )
    mine, own_two = lax.optimization_barrier((mine, own_two))
    theirs = lax.ppermute(mine, "sec", swap)
    both_dims = (2 * rows_two, width_two)
    keep, send = block_call(
        mlp_two_kernel,
        (shape_of(both_dims, jnp.float32), shape_of(both_dims, jnp.float32)),
        (mine, theirs, own_two, bias_two[0]),
        [pltpu.VMEM(both_dims, bfloat), pltpu.VMEM(both_dims, bfloat)],
    )
    back = lax.ppermute(send, "sec", swap)
    features, d_conv_two = block_call(
        two_finish_kernel,
        (shape_of((rows_two, width_two), bfloat), shape_of((rows_two, width_two), bfloat)),
        (keep, back, merged, flat_scale_two, flat_down_two, conv_two, flat_gain_two),
        [],
    )
    back_tile = d_conv_two.reshape(half_rows, half_cols, width_two)
    (d_merged,) = tile_call(
        back_two_kernel,
        (shape_of((rows_two, width_two), bfloat),),
        half_rows,
        half_cols,
        width_two,
        (back_tile, *halo_of(back_tile, 3), kernel_two, grad_rows),
    )
    d_conv_one, upstream_one = block_call(
        back_mlp_one,
        (shape_of((rows_one, width_one), bfloat), shape_of((rows_one, width_one), jnp.float32)),
        (
            d_merged,
            merge_weight,
            section_out,
            flat_gain_mid,
            flat_scale_one,
            own_one,
            other_one,
            slope_own,
            slope_other,
            conv_one,
            flat_gain_one,
        ),
        [
            pltpu.VMEM((rows_one, width_one), bfloat),
            pltpu.VMEM((rows_one, width_one), jnp.float32),
        ],
    )
    d_conv_one = d_conv_one.reshape(tile_rows, 2, half_cols, width_one)
    (input_grad,) = tile_call(
        back_one_kernel,
        (shape_of((tile_rows, tile_cols, width_one), bfloat),),
        tile_rows,
        tile_cols,
        width_one,
        (d_conv_one, *halo_of(d_conv_one, 2), kernel_one, upstream_one),
        (pltpu.VMEM((tile_rows, tile_cols, lanes), jnp.float32),),
    )
    return (
        features.reshape(micro_count, half_rows, half_cols, width_two),
        input_grad.reshape(images.shape),
    )


def solution(mesh):
    in_specs = (
        P("sec", "row", "col", None),
        P(),
        P(),
        P(),
        P(None, ("sec", "row", "col")),
        P(),
        P(None, ("sec", "row", "col")),
        P(),
        P(),
        P(),
        P(),
        P(),
        P(),
        P(),
        P(),
        P(),
        P(None, ("sec", "row", "col")),
        P(),
        P(None, ("sec", "row", "col")),
        P(),
        P(),
        P("sec", "row", "col", None),
    )
    out_specs = (P("sec", "row", "col", None), P("sec", "row", "col", None))
    return jax.shard_map(
        on_device, mesh=mesh, in_specs=in_specs, out_specs=out_specs, check_vma=False
    )
```

```python
import jax
import jax.numpy as jnp
from jax import lax
from jax.experimental import pallas as pl
from jax.experimental.pallas import tpu as pltpu
from jax.sharding import PartitionSpec as P

norm_eps = 1e-06


def exchange(block, axis, dim, width):
    count = lax.axis_size(axis)
    forward = [(i, i + 1) for i in range(count - 1)]
    backward = [(target, source) for source, target in forward]
    low = lax.ppermute(
        lax.slice_in_dim(block, block.shape[dim] - width, None, axis=dim), axis, forward
    )
    high = lax.ppermute(lax.slice_in_dim(block, 0, width, axis=dim), axis, backward)
    return low, high


def halo_of(block, width):
    dim = block.ndim - 2
    top, bottom = exchange(block, "row", 0, 3)

    def edge(first, last):
        parts = [lax.slice_in_dim(part, first, last, axis=dim) for part in (top, block, bottom)]
        return jnp.concatenate(parts, axis=0)

    count = lax.axis_size("col")
    extent = block.shape[dim]
    forward = [(i, i + 1) for i in range(count - 1)]
    backward = [(target, source) for source, target in forward]
    left = lax.ppermute(edge(extent - width, extent), "col", forward)
    right = lax.ppermute(edge(0, width), "col", backward)
    return top, bottom, left, right


def ring_collect(piece, axis, inner, stride):
    count = lax.axis_size(axis)
    own_place = (lax.axis_index(axis) // stride) % inner
    found = jnp.zeros((inner, *piece.shape), piece.dtype)
    found = lax.dynamic_update_index_in_dim(found, piece, own_place, 0)
    for shift in range(1, inner):
        pairs = []
        for target in range(count):
            place = (target // stride) % inner
            source = target + ((place + shift) % inner - place) * stride
            pairs.append((source, target))
        arrived = lax.ppermute(piece, axis, pairs)
        found = lax.dynamic_update_index_in_dim(found, arrived, (own_place + shift) % inner, 0)
    return found


def normal_cdf(values):
    return 0.5 * (1.0 + lax.erf(values * 0.7071067811865476))


def slope_from(values, cdf):
    return cdf + values * jnp.exp(-0.5 * values * values) * 0.3989422804014327


def norm_forward(values, norm_gain, norm_shift):
    center = values - jnp.mean(values, axis=-1, keepdims=True)
    inv_std = lax.rsqrt(jnp.mean(center * center, axis=-1, keepdims=True) + norm_eps)
    scaled = center * inv_std
    return (scaled, inv_std, scaled * norm_gain + norm_shift)


def norm_backward(upstream, scaled, inv_std, norm_gain):
    weighted = upstream * norm_gain
    mean_one = jnp.mean(weighted, axis=-1, keepdims=True)
    mean_two = jnp.mean(weighted * scaled, axis=-1, keepdims=True)
    return inv_std * (weighted - mean_one - scaled * mean_two)


def contract_last(left_side, right_side):
    return lax.dot_general(
        left_side, right_side, (((1,), (1,)), ((), ())), preferred_element_type=jnp.float32
    )


lanes = 128


def fill_rows(frame, source, first, width):
    for row in range(source.shape[0]):
        for tile in range(source.shape[-1] // lanes):
            part = source[row, :, tile * lanes : (tile + 1) * lanes].astype(jnp.float32)
            frame[tile, first + row, 8 : 8 + width, :] = part


def fill_edges(frame, left, right, width):
    for row in range(left.shape[0]):
        for tile in range(left.shape[-1] // lanes):
            span = slice(tile * lanes, (tile + 1) * lanes)
            frame[tile, row, 5:8, :] = left[row, :, span].astype(jnp.float32)
            frame[tile, row, 8 + width : 11 + width, :] = right[row, :, span].astype(jnp.float32)


def fill_parity_rows(frame, source, first):
    halves = source.shape[2]
    for row in range(source.shape[0]):
        for tile in range(source.shape[-1] // lanes):
            for parity in range(2):
                part = source[row, parity, :, tile * lanes : (tile + 1) * lanes]
                frame[tile, first + row, pl.ds(8 + parity, halves, stride=2), :] = part.astype(
                    jnp.float32
                )


def fill_parity_edges(frame, left, right, width):
    for row in range(left.shape[0]):
        for tile in range(left.shape[-1] // lanes):
            span = slice(tile * lanes, (tile + 1) * lanes)
            for parity in range(2):
                for half in range(2):
                    col = 2 * half + parity
                    frame[tile, row, 4 + col : 5 + col, :] = left[
                        row, parity, half : half + 1, span
                    ].astype(jnp.float32)
                    frame[tile, row, 8 + width + col : 9 + width + col, :] = right[
                        row, parity, half : half + 1, span
                    ].astype(jnp.float32)


def depthwise(frame, taps, tile, rows, cols, first, stride, flipped):
    sums = [jnp.zeros((cols, lanes), jnp.float32) for _ in range(rows)]
    span = pl.ds(pl.multiple_of(tile * lanes, lanes), lanes)
    for tap_col in range(7):
        weights = [taps[pl.ds(7 * tap_row + tap_col, 1), span] for tap_row in range(7)]
        start = 5 + first + (6 - tap_col if flipped else tap_col)
        for row in range(rows + 6):
            if stride == 1:
                values = frame[tile, row, pl.ds(start, cols), :]
            else:
                values = frame[tile, row, pl.ds(start, cols, stride=stride), :]
            for tap_row in range(7):
                target = row - (6 - tap_row if flipped else tap_row)
                if 0 <= target < rows:
                    sums[target] = sums[target] + values * weights[tap_row]
    return sums


def norm_rows(values_ref, normed_ref, gain_ref, shift_ref, chunk):
    gain = gain_ref[...]
    shift = shift_ref[...]

    for first in range(0, values_ref.shape[0], chunk):
        span = slice(first, first + chunk)
        values = values_ref[span, :].astype(jnp.float32)
        normed_ref[span, :] = norm_forward(values, gain, shift)[2].astype(normed_ref.dtype)


def conv_one_kernel(
    tile_ref, top, bottom, left, right, taps, gain, shift, normed, conv, residual, frame
):
    rows, width, channels = tile_ref.shape
    halves = width // 2
    fill_rows(frame, top, 0, width)
    fill_rows(frame, tile_ref, 3, width)
    fill_rows(frame, bottom, 3 + rows, width)
    fill_edges(frame, left, right, width)

    def step(tile, carry):
        span = pl.ds(pl.multiple_of(tile * lanes, lanes), lanes)
        for parity in range(2):
            sums = depthwise(frame, taps, tile, rows, halves, parity, 2, False)
            for row in range(rows):
                place = pl.ds(row * width + parity * halves, halves)
                conv[place, span] = sums[row]
                own = frame[tile, 3 + row, pl.ds(8 + parity, halves, stride=2), :]
                residual[place, span] = own.astype(residual.dtype)
        return carry

    lax.fori_loop(0, channels // lanes, step, 0)
    norm_rows(conv, normed, gain, shift, 32)


def back_one_kernel(tile_ref, top, bottom, left, right, taps, upstream, out, frame, total):
    rows, _, halves, channels = tile_ref.shape
    width = 2 * halves
    fill_parity_rows(frame, top, 0)
    fill_parity_rows(frame, tile_ref, 3)
    fill_parity_rows(frame, bottom, 3 + rows)
    fill_parity_edges(frame, left, right, width)

    def step(tile, carry):
        span = pl.ds(pl.multiple_of(tile * lanes, lanes), lanes)
        for parity in range(2):
            sums = depthwise(frame, taps, tile, rows, halves, parity, 2, True)
            for row in range(rows):
                place = pl.ds(row * width + parity * halves, halves)
                total[row, pl.ds(parity, halves, stride=2), :] = sums[row] + upstream[place, span]
        for row in range(rows):
            out[row, :, span] = total[row].astype(out.dtype)
        return carry

    lax.fori_loop(0, channels // lanes, step, 0)


def conv_two_kernel(
    tile_ref, top, bottom, left, right, taps, gain, shift, grad, scale, mine, conv, frame
):
    rows, width, channels = tile_ref.shape
    fill_rows(frame, top, 0, width)
    fill_rows(frame, tile_ref, 3, width)
    fill_rows(frame, bottom, 3 + rows, width)
    fill_edges(frame, left, right, width)

    def step(tile, carry):
        span = pl.ds(pl.multiple_of(tile * lanes, lanes), lanes)
        sums = depthwise(frame, taps, tile, rows, width, 0, 1, False)
        for row in range(rows):
            conv[pl.ds(row * width, width), span] = sums[row].astype(conv.dtype)
        return carry

    lax.fori_loop(0, channels // lanes, step, 0)
    norm_rows(conv, mine, gain, shift, 32)
    count = rows * width
    mine[count:, :] = (grad[...].astype(jnp.float32) * scale[...]).astype(mine.dtype)


def back_two_kernel(tile_ref, top, bottom, left, right, taps, grad, out, frame):
    rows, width, channels = tile_ref.shape
    fill_rows(frame, top, 0, width)
    fill_rows(frame, tile_ref, 3, width)
    fill_rows(frame, bottom, 3 + rows, width)
    fill_edges(frame, left, right, width)

    def step(tile, carry):
        span = pl.ds(pl.multiple_of(tile * lanes, lanes), lanes)
        sums = depthwise(frame, taps, tile, rows, width, 0, 1, True)
        for row in range(rows):
            place = pl.ds(row * width, width)
            d_taps = sums[row].astype(jnp.bfloat16).astype(jnp.float32)
            out[place, span] = (d_taps + grad[place, span].astype(jnp.float32)).astype(out.dtype)
        return carry

    lax.fori_loop(0, channels // lanes, step, 0)


def dot(left_side, right_side):
    return jnp.dot(left_side, right_side, preferred_element_type=jnp.float32)


def row_blocks(total, size):
    size = min(total, size)
    return [slice(first, first + size) for first in range(0, total, size)]


hidden_block = 256


def over_hidden(weights, step, together=1):
    total = weights.shape[0]
    block = min(total, hidden_block)
    together = min(together, total // block)

    def run(index, carry):
        for part in range(together):
            place = index * together + part
            step(place, pl.ds(pl.multiple_of(place * block, block), block))
        return carry

    lax.fori_loop(0, total // block // together, run, 0)


def mlp_one_half(normed, weights, bias, branch):
    width = normed.shape[1]
    branch[...] = jnp.zeros_like(branch)

    def step(place, units):
        for rows in row_blocks(normed.shape[0], 256):
            pre_act = contract_last(normed[rows, :], weights[units, :width]) + bias[:, units]
            hidden = (pre_act * normal_cdf(pre_act)).astype(jnp.bfloat16)
            branch[rows, :] += dot(hidden, weights[units, width:])

    over_hidden(weights, step)


def mlp_one_finish(
    normed, weights, bias, partial, residual, down_bias, scale, gain, shift, merge, merge_bias,
    section, merged, branch, patches,
):
    mlp_one_half(normed, weights, bias, branch)
    positions, width = normed.shape
    quarter = patches.shape[0]
    half_cols = patches.shape[2]
    step_rows = 4 * half_cols

    for index in range(quarter):
        rows = slice(index * step_rows, (index + 1) * step_rows)
        total = branch[rows, :] + partial[rows, :] + down_bias[...]
        out = (residual[rows, :].astype(jnp.float32) + scale[...] * total).astype(jnp.bfloat16)
        section[rows, :] = out
        normal = norm_forward(out.astype(jnp.float32), gain[...], shift[...])[2]
        normal = normal.astype(jnp.bfloat16)
        for place in range(4):
            patches[index, place] = normal[place * half_cols : (place + 1) * half_cols, :]

    total = merge_bias[...]
    for place in range(4):
        patch = patches[:, place].reshape(quarter * half_cols, width)
        total = total + dot(patch, merge[place * width : (place + 1) * width, :])
    merged[...] = total.astype(merged.dtype)


def slope_one_kernel(normed, own, other, bias_own, bias_other, slope_own, slope_other):
    width = normed.shape[1]

    def step(place, units):
        for rows in row_blocks(normed.shape[0], 256):
            for weights, bias, slope in (
                (own, bias_own, slope_own),
                (other, bias_other, slope_other),
            ):
                pre_act = contract_last(normed[rows, :], weights[units, :width]) + bias[:, units]
                slope[place, rows, :] = slope_from(pre_act, normal_cdf(pre_act)).astype(
                    slope.dtype
                )

    over_hidden(own, step)


def back_mlp_one(
    d_merged, merge, section, gain_mid, scale, own, other, slope_own, slope_other, conv, gain,
    d_conv, upstream, d_branch, d_normed,
):
    width = section.shape[1]
    quarter = d_merged.shape[0]
    groups = section.shape[0] // 64
    half_cols = quarter // groups
    for place in range(4):
        d_normal = contract_last(d_merged[...], merge[place * width : (place + 1) * width, :])
        for group in range(groups):
            first = (4 * group + place) * half_cols
            rows = slice(first, first + half_cols)
            scaled, inv_std, _ = norm_forward(section[rows, :].astype(jnp.float32), 1.0, 0.0)
            flow = norm_backward(
                d_normal[group * half_cols : (group + 1) * half_cols],
                scaled,
                inv_std,
                gain_mid[...],
            )
            upstream[rows, :] = flow
            d_branch[rows, :] = (flow * scale[...]).astype(d_branch.dtype)
    d_normed[...] = jnp.zeros_like(d_normed)

    def step(place, units):
        for rows in row_blocks(section.shape[0], 256):
            total = d_normed[rows, :]
            for weights, slope in ((own, slope_own), (other, slope_other)):
                d_hidden = contract_last(d_branch[rows, :], weights[units, width:])
                d_pre = (d_hidden * slope[place, rows, :].astype(jnp.float32)).astype(jnp.bfloat16)
                total = total + dot(d_pre, weights[units, :width])
            d_normed[rows, :] = total

    over_hidden(own, step)
    norm_back_rows(conv, d_normed, gain, d_conv, 32)


def norm_back_rows(conv, d_normed, gain, d_conv, chunk):
    for first in range(0, conv.shape[0], chunk):
        rows = slice(first, first + chunk)
        scaled, inv_std, _ = norm_forward(conv[rows, :].astype(jnp.float32), 1.0, 0.0)
        flow = norm_backward(d_normed[rows, :], scaled, inv_std, gain[...])
        d_conv[rows, :] = flow.astype(d_conv.dtype)


def mlp_two_kernel(mine, theirs, weights, bias, keep, send, stacked, d_stacked):
    count = mine.shape[0] // 2
    width = mine.shape[1]
    for first, source in ((0, mine), (count, theirs)):
        stacked[first : first + count, :] = source[:count, :]
        d_stacked[first : first + count, :] = source[count:, :]
    keep[...] = jnp.zeros_like(keep)
    send[...] = jnp.zeros_like(send)

    def step(place, units):
        pre_act = contract_last(stacked[...], weights[units, :width]) + bias[:, units]
        d_hidden = contract_last(d_stacked[...], weights[units, width:])
        cdf = normal_cdf(pre_act)
        hidden = (pre_act * cdf).astype(jnp.bfloat16)
        d_pre = (d_hidden * slope_from(pre_act, cdf)).astype(jnp.bfloat16)
        branch = dot(hidden, weights[units, width:])
        d_normed = dot(d_pre, weights[units, :width])
        keep[:count, :] += branch[:count]
        send[:count, :] += branch[count:]
        keep[count:, :] += d_normed[:count]
        send[count:, :] += d_normed[count:]

    over_hidden(weights, step, 2)


def two_finish_kernel(keep, back, merged, scale, down_bias, conv, gain, features, d_conv):
    count = merged.shape[0]

    for first in range(0, count, 32):
        rows = slice(first, first + 32)
        low = slice(count + first, count + first + 32)
        total = keep[rows, :] + back[rows, :] + down_bias[...]
        out = merged[rows, :].astype(jnp.float32) + scale[...] * total
        features[rows, :] = out.astype(features.dtype)
        scaled, inv_std, _ = norm_forward(conv[rows, :].astype(jnp.float32), 1.0, 0.0)
        flow = norm_backward(keep[low, :] + back[low, :], scaled, inv_std, gain[...])
        d_conv[rows, :] = flow.astype(d_conv.dtype)


megabyte = 1024 * 1024


def shape_of(dims, dtype):
    return jax.ShapeDtypeStruct(dims, dtype)


def block_call(kernel, outputs, operands, scratch, limit=48):
    whole = pl.BlockSpec(memory_space=pltpu.VMEM)
    return pl.pallas_call(
        kernel,
        out_shape=outputs,
        in_specs=[whole] * len(operands),
        out_specs=[whole] * len(outputs),
        scratch_shapes=scratch,
        compiler_params=pltpu.CompilerParams(vmem_limit_bytes=limit * megabyte),
    )(*operands)


def tile_call(kernel, outputs, rows, width, channels, operands, extra=()):
    frame = pltpu.VMEM((channels // lanes, rows + 6, width + 16, lanes), jnp.float32)
    return block_call(kernel, outputs, operands, [frame, *extra])


def on_device(
    images,
    kernel_one,
    gain_one,
    shift_one,
    up_one,
    up_bias_one,
    down_one,
    down_bias_one,
    scale_one,
    gain_mid,
    shift_mid,
    merge_weight,
    merge_bias,
    kernel_two,
    gain_two,
    shift_two,
    up_two,
    up_bias_two,
    down_two,
    down_bias_two,
    scale_two,
    grad_out,
):
    micro_count, tile_rows, tile_cols, width_one = images.shape
    width_two = merge_weight.shape[1]
    half_rows = tile_rows // 2
    half_cols = tile_cols // 2
    rows_one = micro_count * tile_rows * tile_cols
    rows_two = micro_count * half_rows * half_cols

    swap = [(0, 1), (1, 0)]
    side = lax.axis_index("sec")
    row_count = lax.axis_size("row")
    col_count = lax.axis_size("col")
    inner = 4 if row_count % 4 == 0 else row_count
    outer = row_count // inner
    bfloat = jnp.bfloat16

    def bias_halves(bias):
        halves = bias.reshape(2, 1, -1)
        return (
            jnp.where(side == 0, halves[0], halves[1]),
            jnp.where(side == 0, halves[1], halves[0]),
        )

    share_two = up_two.shape[1]
    packed_one = jnp.concatenate([up_one.T, down_one.T], axis=1)
    packed = jnp.concatenate([up_two.T, down_two.T, packed_one], axis=0)
    pair = 2 if col_count % 2 == 0 else 1
    column = ring_collect(ring_collect(packed, "col", pair, 1), "col", col_count // pair, pair)
    column = column.reshape(col_count, *packed.shape)
    part_one = column[:, 2 * share_two :].reshape(-1, 2 * width_one)
    part_two = jnp.concatenate(
        [
            column[:, :share_two].reshape(-1, width_two),
            column[:, share_two : 2 * share_two].reshape(-1, width_two),
        ],
        axis=1,
    )
    own_two = lax.all_gather(part_two, "row", axis=0, tiled=True)
    own_one = ring_collect(part_one, "row", inner, 1).reshape(-1, 2 * width_one)
    own_one = ring_collect(own_one, "row", outer, inner).reshape(-1, 2 * width_one)
    bias_one = bias_halves(up_bias_one)
    bias_two = bias_halves(up_bias_two)

    image_tile = images.reshape(tile_rows, tile_cols, width_one)
    normed_one, conv_one, images_par = tile_call(
        conv_one_kernel,
        (
            shape_of((rows_one, width_one), bfloat),
            shape_of((rows_one, width_one), jnp.float32),
            shape_of((rows_one, width_one), bfloat),
        ),
        tile_rows,
        tile_cols,
        width_one,
        (image_tile, *halo_of(image_tile, 3), kernel_one, gain_one[None], shift_one[None]),
    )
    flat = tuple(
        vector[None]
        for vector in (
            down_bias_one, scale_one, gain_mid, shift_mid, merge_bias, gain_two, shift_two,
            scale_two, down_bias_two, gain_one,
        )
    )
    own_one, normed_one, images_par, bias_one, bias_two, flat = lax.optimization_barrier(
        (own_one, normed_one, images_par, bias_one, bias_two, flat)
    )
    (
        flat_down_one, flat_scale_one, flat_gain_mid, flat_shift_mid, flat_merge_bias,
        flat_gain_two, flat_shift_two, flat_scale_two, flat_down_two, flat_gain_one,
    ) = flat
    other_one = lax.ppermute(own_one, "sec", swap)

    (partial_one,) = block_call(
        mlp_one_half,
        (shape_of((rows_one, width_one), jnp.float32),),
        (normed_one, own_one, bias_one[0]),
        [],
    )
    section_out, merged = block_call(
        mlp_one_finish,
        (shape_of((rows_one, width_one), bfloat), shape_of((rows_two, width_two), bfloat)),
        (
            normed_one,
            other_one,
            bias_one[1],
            partial_one,
            images_par,
            flat_down_one,
            flat_scale_one,
            flat_gain_mid,
            flat_shift_mid,
            merge_weight,
            flat_merge_bias,
        ),
        [
            pltpu.VMEM((rows_one, width_one), jnp.float32),
            pltpu.VMEM((micro_count * half_rows, 4, half_cols, width_one), bfloat),
        ],
    )
    block = min(own_one.shape[0], hidden_block)
    slope_dims = (own_one.shape[0] // block, rows_one, block)
    slope_own, slope_other = block_call(
        slope_one_kernel,
        (shape_of(slope_dims, bfloat), shape_of(slope_dims, bfloat)),
        (normed_one, own_one, other_one, *bias_one),
        [],
    )

    merged_tile = merged.reshape(half_rows, half_cols, width_two)
    grad_rows = grad_out.reshape(rows_two, width_two)
    mine, conv_two = tile_call(
        conv_two_kernel,
        (shape_of((2 * rows_two, width_two), bfloat), shape_of((rows_two, width_two), bfloat)),
        half_rows,
        half_cols,
        width_two,
        (
            merged_tile,
            *halo_of(merged_tile, 3),
            kernel_two,
            flat_gain_two,
            flat_shift_two,
            grad_rows,
            flat_scale_two,
        ),
    )
    mine, own_two = lax.optimization_barrier((mine, own_two))
    theirs = lax.ppermute(mine, "sec", swap)
    both_dims = (2 * rows_two, width_two)
    keep, send = block_call(
        mlp_two_kernel,
        (shape_of(both_dims, jnp.float32), shape_of(both_dims, jnp.float32)),
        (mine, theirs, own_two, bias_two[0]),
        [pltpu.VMEM(both_dims, bfloat), pltpu.VMEM(both_dims, bfloat)],
    )
    back = lax.ppermute(send, "sec", swap)
    features, d_conv_two = block_call(
        two_finish_kernel,
        (shape_of((rows_two, width_two), bfloat), shape_of((rows_two, width_two), bfloat)),
        (keep, back, merged, flat_scale_two, flat_down_two, conv_two, flat_gain_two),
        [],
    )
    back_tile = d_conv_two.reshape(half_rows, half_cols, width_two)
    (d_merged,) = tile_call(
        back_two_kernel,
        (shape_of((rows_two, width_two), bfloat),),
        half_rows,
        half_cols,
        width_two,
        (back_tile, *halo_of(back_tile, 3), kernel_two, grad_rows),
    )
    d_conv_one, upstream_one = block_call(
        back_mlp_one,
        (shape_of((rows_one, width_one), bfloat), shape_of((rows_one, width_one), jnp.float32)),
        (
            d_merged,
            merge_weight,
            section_out,
            flat_gain_mid,
            flat_scale_one,
            own_one,
            other_one,
            slope_own,
            slope_other,
            conv_one,
            flat_gain_one,
        ),
        [
            pltpu.VMEM((rows_one, width_one), bfloat),
            pltpu.VMEM((rows_one, width_one), jnp.float32),
        ],
    )
    d_conv_one = d_conv_one.reshape(tile_rows, 2, half_cols, width_one)
    (input_grad,) = tile_call(
        back_one_kernel,
        (shape_of((tile_rows, tile_cols, width_one), bfloat),),
        tile_rows,
        tile_cols,
        width_one,
        (d_conv_one, *halo_of(d_conv_one, 2), kernel_one, upstream_one),
        (pltpu.VMEM((tile_rows, tile_cols, lanes), jnp.float32),),
    )
    return (
        features.reshape(micro_count, half_rows, half_cols, width_two),
        input_grad.reshape(images.shape),
    )


def solution(mesh):
    in_specs = (
        P("sec", "row", "col", None),
        P(),
        P(),
        P(),
        P(None, ("sec", "row", "col")),
        P(),
        P(None, ("sec", "row", "col")),
        P(),
        P(),
        P(),
        P(),
        P(),
        P(),
        P(),
        P(),
        P(),
        P(None, ("sec", "row", "col")),
        P(),
        P(None, ("sec", "row", "col")),
        P(),
        P(),
        P("sec", "row", "col", None),
    )
    out_specs = (P("sec", "row", "col", None), P("sec", "row", "col", None))
    return jax.shard_map(
        on_device, mesh=mesh, in_specs=in_specs, out_specs=out_specs, check_vma=False
    )
```
